256 devices in a mesh: row: 16 (over z, core), col: 16 (over y, x).
Axes of the slice: x: 4, y: 4, z: 8, core: 2. Of those that a mesh axis runs over, the one named last changes fastest.
Arguments:
- teacher_image: bfloat16 [16384, 1024], P(('row', 'col')), may hold values from -1 to 1
- teacher_text: bfloat16 [16384, 1024], P(('row', 'col')), may hold values from -1 to 1
- student_image: bfloat16 [16384, 1024], P(('row', 'col')), may hold values from -1 to 1
- student_text: bfloat16 [16384, 1024], P(('row', 'col')), may hold values from -1 to 1
Outputs:
- image_grad: bfloat16 [16384, 1024], P(('row', 'col'))
- text_grad: bfloat16 [16384, 1024], P(('row', 'col'))
- loss: float32 [], replicated
The draws below stay inside these ranges and needn't reach their ends.
All inputs are finite; a program needn't handle non-finite values.
Results may differ from the reference program's by a relative error of at most 0.0048.
Values may be sent and summed in bfloat16 or wider, within the bound.
No kernel may reach another device: no remote copies, remote signals or barrier semaphores. Data moves between devices by JAX's collectives and lax.ppermute only.
A program may use at most 64 MiB of HBM per device.

```python
import jax
import jax.numpy as jnp
from jax import lax

D = 1024
B = 16384


def embed_pair(key, salt, spread):
    key = jax.random.fold_in(key, salt)
    keys = jax.random.split(key, 6)
    image = jnp.clip(jax.random.normal(keys[0], (B, D), jnp.float32), -5.0, 5.0) * D ** (-0.5)
    text = jnp.clip(jax.random.normal(keys[1], (B, D), jnp.float32), -5.0, 5.0) * D ** (-0.5)
    image = image * jnp.exp(jax.random.uniform(keys[2], (B, 1), jnp.float32, -spread, spread))
    text = text * jnp.exp(jax.random.uniform(keys[3], (B, 1), jnp.float32, -spread, spread))
    picks = jax.random.randint(keys[4], (4,), 0, B)
    targets = jax.random.randint(keys[5], (4,), 0, B)
    image = image.at[picks].set(image[picks])
    near = (picks + 1) % B
    image = image.at[near].set(image[near])
    text = text.at[targets].set(text[targets])
    after = (targets + 1) % B
    text = text.at[after].set(text[after])
    return (jnp.clip(image, -1.0, 1.0), jnp.clip(text, -1.0, 1.0))


def draw_teacher_image(key, part):
    spread = 0.0
    return embed_pair(key, 11, spread)[0].astype(jnp.bfloat16)


def draw_teacher_text(key, part):
    spread = 0.0
    return embed_pair(key, 11, spread)[1].astype(jnp.bfloat16)


def draw_student_image(key, part):
    spread = 0.0
    return embed_pair(key, 23, spread)[0].astype(jnp.bfloat16)


def draw_student_text(key, part):
    spread = 0.0
    return embed_pair(key, 23, spread)[1].astype(jnp.bfloat16)


def setup_inputs(seed: int = 0) -> dict:
    streams_of = jax.random.split(jax.random.key(seed), 5)
    teacher_image = draw_teacher_image(jax.random.fold_in(streams_of[4], 71), 0)
    teacher_text = draw_teacher_text(jax.random.fold_in(streams_of[4], 71), 0)
    student_image = draw_student_image(jax.random.fold_in(streams_of[4], 71), 0)
    student_text = draw_student_text(jax.random.fold_in(streams_of[4], 71), 0)
    return dict(teacher_image=teacher_image, teacher_text=teacher_text, student_image=student_image, student_text=student_text)


def logits_of(left, right):
    return 100.0 * jnp.dot(left, right.T, preferred_element_type=jnp.float32)


def row_lse(values):
    top = jnp.max(values, axis=1)
    return top + jnp.log(jnp.sum(jnp.exp(values - top[:, None]), axis=1))


def fold_columns(top, total, values):
    block_top = jnp.max(values, axis=0)
    new_top = jnp.maximum(top, block_top)
    new_total = total * jnp.exp(top - new_top) + jnp.sum(jnp.exp(values - new_top[None, :]), axis=0)
    return new_top, new_total


def reference(teacher_image, teacher_text, student_image, student_text):
    count = teacher_image.shape[0]
    width = teacher_image.shape[1]
    block = min(1024, count)
    blocks = count // block
    t_img = teacher_image.reshape(blocks, block, width)
    s_img = student_image.reshape(blocks, block, width)

    def first(carry, pieces):
        ti, si = pieces
        teach = logits_of(ti, teacher_text)
        learn = logits_of(si, student_text)
        ct_top, ct_total = fold_columns(carry[0], carry[1], teach)
        cs_top, cs_total = fold_columns(carry[2], carry[3], learn)
        return (ct_top, ct_total, cs_top, cs_total), (row_lse(teach), row_lse(learn))

    low = jnp.full((count,), -jnp.inf, jnp.float32)
    zero = jnp.zeros((count,), jnp.float32)
    carry, rows = lax.scan(first, (low, zero, low, zero), (t_img, s_img))
    col_t = carry[0] + jnp.log(carry[1])
    col_s = carry[2] + jnp.log(carry[3])

    def second(state, pieces):
        ti, si, rt, rs = pieces
        teach = logits_of(ti, teacher_text)
        learn = logits_of(si, student_text)
        gap = teach - learn
        p_row = jnp.exp(teach - rt[:, None])
        q_row = jnp.exp(learn - rs[:, None])
        p_col = jnp.exp(teach - col_t[None, :])
        q_col = jnp.exp(learn - col_s[None, :])
        part = jnp.sum((p_row + p_col) * gap) + jnp.sum(rs - rt)
        coupling = (0.5 * (q_row - p_row + q_col - p_col)).astype(jnp.bfloat16)
        img = (100.0 * jnp.dot(coupling, student_text, preferred_element_type=jnp.float32)).astype(jnp.bfloat16)
        txt = state[0] + 100.0 * jnp.dot(coupling.T, si, preferred_element_type=jnp.float32)
        return (txt, state[1] + part), img

    start = (jnp.zeros((count, width), jnp.float32), jnp.zeros((), jnp.float32))
    state, img_blocks = lax.scan(second, start, (t_img, s_img, rows[0], rows[1]))
    loss = (state[1] + jnp.sum(col_s - col_t)) * (0.5 / count)
    image_grad = img_blocks.reshape(count, width)
    text_grad = state[0].astype(jnp.bfloat16)
    return image_grad, text_grad, loss
```

```python
import jax
import jax.numpy as jnp
from jax import lax
from jax.sharding import PartitionSpec as P

NX, NY, NZ, NC = 4, 4, 8, 2
BF = jnp.bfloat16
F32 = jnp.float32


def move_x(v, d):
    return lax.ppermute(
        v, "col", [(y * NX + x, y * NX + (x + d) % NX) for y in range(NY) for x in range(NX)]
    )


def move_y(v, d):
    return lax.ppermute(
        v, "col", [(y * NX + x, (y + d) % NY * NX + x) for y in range(NY) for x in range(NX)]
    )


def move_z(v, d):
    return lax.ppermute(
        v, "row", [(z * NC + c, (z + d) % NZ * NC + c) for z in range(NZ) for c in range(NC)]
    )


def move_c(v):
    return lax.ppermute(
        v, "row", [(z * NC + c, z * NC + 1 - c) for z in range(NZ) for c in range(NC)]
    )


def ring4_gather(move, v):
    half = v.shape[0] // 2
    back = move(v, 1)
    ahead = move(v, -1)
    far_a = move(back[:half], 1)
    far_b = move(ahead[half:], -1)
    return [v, ahead, jnp.concatenate([far_a, far_b], axis=0), back]


def gather_xy(first, second, v):
    line = jnp.concatenate(ring4_gather(first, v), axis=0)
    return ring4_gather(second, line)


def gather_zc(v):
    n = v.shape[0] // 2
    fwd, bwd = [v], [v]
    for _ in range(3):
        fwd.append(move_z(fwd[-1], 1))
        bwd.append(move_z(bwd[-1], -1))
    far_a = move_z(fwd[3][:n], 1)
    far_b = move_z(bwd[3][n:], -1)
    far = jnp.concatenate([far_a, far_b], axis=0)
    blocks = [v, bwd[1], bwd[2], bwd[3], far, fwd[3], fwd[2], fwd[1]]
    out = []
    for b in blocks:
        out += [b, move_c(b)]
    teacher = jnp.concatenate([b[:n] for b in out], axis=0)
    student = jnp.concatenate([b[n:] for b in out], axis=0)
    return teacher, student


def similarity(left, right):
    return 100.0 * lax.dot_general(
        left, right, (((1,), (1,)), ((), ())), preferred_element_type=F32
    )


def local_stats(teach, learn, gap, axis):
    t_top = jnp.max(teach, axis=axis, keepdims=True)
    s_top = jnp.max(learn, axis=axis, keepdims=True)
    e = jnp.exp(teach - t_top)
    t_sum = jnp.sum(e, axis=axis)
    w = jnp.sum(e * gap, axis=axis)
    s_sum = jnp.sum(jnp.exp(learn - s_top), axis=axis)
    return jnp.stack([t_top.reshape(-1), t_sum, s_top.reshape(-1), s_sum, w])


def merge(parts):
    t_top = parts[0][0]
    s_top = parts[0][2]
    for p in parts[1:]:
        t_top = jnp.maximum(t_top, p[0])
        s_top = jnp.maximum(s_top, p[2])
    t_sum = s_sum = w = 0.0
    for p in parts:
        a = jnp.exp(p[0] - t_top)
        t_sum = t_sum + p[1] * a
        w = w + p[4] * a
        s_sum = s_sum + p[3] * jnp.exp(p[2] - s_top)
    return jnp.stack([t_top, t_sum, s_top, s_sum, w])


def merge_ring4(move, st, axis):
    parts = [st]
    for s in (1, 2, 3):
        parts.append(jnp.roll(move(st, s), -s, axis=axis))
    return merge(parts)


def merge_z(st):
    for s in (1, 2, 4):
        st = merge([st, jnp.roll(move_z(st, s), -s, axis=1)])
    return st


def ring4_reduce(move, v):
    half = v.shape[1] // 2
    a = move(v[2, :half].astype(BF), 1)
    b = move(v[2, half:].astype(BF), -1)
    up = jnp.concatenate([v[1, :half] + a.astype(F32), v[1, half:]], axis=0).astype(BF)
    down = jnp.concatenate([v[3, :half], v[3, half:] + b.astype(F32)], axis=0).astype(BF)
    r_up = move(up, 1)
    r_down = move(down, -1)
    return v[0] + r_up.astype(F32) + r_down.astype(F32)


def reduce_zc(v):
    v = v[:, 0] + move_c(v[:, 1].astype(BF)).astype(F32)
    half = v.shape[1] // 2
    a = move_z(v[4, :half].astype(BF), 1)
    b = move_z(v[4, half:].astype(BF), -1)
    up = jnp.concatenate([v[3, :half] + a.astype(F32), v[3, half:]], axis=0).astype(BF)
    down = jnp.concatenate([v[5, :half], v[5, half:] + b.astype(F32)], axis=0).astype(BF)
    for k in (2, 1):
        up = (v[k] + move_z(up, 1).astype(F32)).astype(BF)
        down = (v[8 - k] + move_z(down, -1).astype(F32)).astype(BF)
    return v[0] + move_z(up, 1).astype(F32) + move_z(down, -1).astype(F32)


def per_device(teacher_image, teacher_text, student_image, student_text):
    n, d = teacher_image.shape
    total_pairs = n * NX * NY * NZ * NC
    t_parts = gather_xy(move_x, move_y, teacher_image)
    s_parts = gather_xy(move_y, move_x, student_image)
    t_cols, s_cols = gather_zc(jnp.concatenate([teacher_text, student_text], axis=0))
    t_rows = jnp.concatenate(t_parts, axis=0)
    s_rows = jnp.stack([p.reshape(NY, n, d) for p in s_parts], axis=1).reshape(NY * NX * n, d)
    teach = similarity(t_rows, t_cols)
    learn = similarity(s_rows, s_cols)
    gap = teach - learn
    row_st = local_stats(teach, learn, gap, 1).reshape(5, NY, NX, n)
    col_st = local_stats(teach, learn, gap, 0).reshape(5, NZ, NC, n)
    row_st = merge_ring4(move_x, row_st, 2)
    row_st = merge_ring4(move_y, row_st, 1)
    col_st = merge([col_st, move_c(col_st)[:, :, ::-1]])
    col_st = merge_z(col_st)
    row_st = row_st.reshape(5, -1)
    col_st = col_st.reshape(5, -1)
    row_t = row_st[0] + jnp.log(row_st[1])
    row_s = row_st[2] + jnp.log(row_st[3])
    col_t = col_st[0] + jnp.log(col_st[1])
    col_s = col_st[2] + jnp.log(col_st[3])
    part_r = jnp.sum(row_st[4] / row_st[1] + (row_s - row_t))
    part_c = jnp.sum(col_st[4] / col_st[1] + (col_s - col_t))
    lr = jnp.full((8, 128), part_r, F32)
    lr = lr + move_c(lr)
    for s in (1, 2, 4):
        lr = lr + move_z(lr, s)
    lc = jnp.full((8, 128), part_c, F32)
    for mv in (move_x, move_y):
        for s in (1, 2):
            lc = lc + mv(lc, s)
    loss = (lr[0, 0] + lc[0, 0]) * (0.5 / total_pairs)
    coupling = 0.5 * (
        jnp.exp(learn - row_s[:, None])
        - jnp.exp(teach - row_t[:, None])
        + jnp.exp(learn - col_s[None, :])
        - jnp.exp(teach - col_t[None, :])
    )
    coupling = coupling.astype(BF)
    text = 100.0 * lax.dot_general(
        coupling, s_rows, (((0,), (0,)), ((), ())), preferred_element_type=F32
    )
    text_grad = reduce_zc(text.reshape(NZ, NC, n, d))
    image = 100.0 * jnp.dot(coupling, s_cols, preferred_element_type=F32)
    image = image.reshape(NY, NX, n, d)
    h = d // 2
    left = image[..., :h].transpose(1, 0, 2, 3).reshape(NX, NY * n, h)
    right = image[..., h:].reshape(NY, NX * n, h)
    left = ring4_reduce(move_y, ring4_reduce(move_x, left).reshape(NY, n, h))
    right = ring4_reduce(move_x, ring4_reduce(move_y, right).reshape(NX, n, h))
    image_grad = jnp.concatenate([left, right], axis=1)
    return (image_grad.astype(BF), text_grad.astype(BF), loss)


def solution(mesh):
    placed = P(("row", "col"), None)
    return jax.shard_map(
        per_device,
        mesh=mesh,
        in_specs=(placed,) * 4,
        out_specs=(placed, placed, P()),
        check_vma=False,
    )
```

```python
import jax
import jax.numpy as jnp
from jax import lax
from jax.sharding import PartitionSpec as P

NX, NY, NZ, NC = 4, 4, 8, 2
BF = jnp.bfloat16
F32 = jnp.float32


def place(z, c, y, x):
    return ((z % NZ * NC + c) * NY + y % NY) * NX + x % NX


def send(v, target):
    pairs = [
        (place(z, c, y, x), place(*target(z, c, y, x)))
        for z in range(NZ)
        for c in range(NC)
        for y in range(NY)
        for x in range(NX)
    ]
    return lax.ppermute(v, ("row", "col"), pairs)


def move_c(v):
    return send(v, lambda z, c, y, x: (z, 1 - c, y, x))


def move_x(v, d):
    return send(v, lambda z, c, y, x: (z, c, y, x + d))


def move_y(v, d):
    return send(v, lambda z, c, y, x: (z, c, y + d, x))


def move_first(v, d):
    return send(v, lambda z, c, y, x: (z, c, y + d * c, x + d * (1 - c)))


def move_second(v, d):
    return send(v, lambda z, c, y, x: (z, c, y + d * (1 - c), x + d * c))


def move_z(v, d):
    return send(v, lambda z, c, y, x: (z + d * (1 - 2 * c), c, y, x))


def gather_rows(v):
    _, n, d = v.shape
    from_m = move_first(v, 1)
    from_p = move_first(v, -1)
    from_2 = move_first(v, 2)
    line = jnp.stack([v, from_p, from_2, from_m], axis=1)
    up = move_second(line, 1)
    down = move_second(line, -1)
    far_a = move_second(up[:, :2], 1)
    far_b = move_second(down[:, 2:], -1)
    got_0 = move_c(line[1])
    got_1 = move_c(jnp.stack([down[1], up[1]]))
    got_2 = move_c(jnp.concatenate([far_a[1], far_b[1]]))
    mine = jnp.stack([line[0], down[0], jnp.concatenate([far_a[0], far_b[0]]), up[0]])
    got = jnp.stack([got_0, got_1[0], got_2, got_1[1]])
    return mine, got


def gather_cols(v):
    out = [v]
    for _ in range(3):
        out.append(move_z(out[-1], 1))
    far = move_z(out[3][0], 1)
    back = [move_c(b) for b in out[1:]]
    far_sib = move_c(far)
    blocks = out + [jnp.stack([far, far_sib])] + [b[::-1] for b in back[::-1]]
    t = jnp.concatenate([b[c, 0] for b in blocks for c in range(2)])
    s = jnp.concatenate([b[c, 1] for b in blocks for c in range(2)])
    return t, s


def similarity(left, right):
    return 100.0 * lax.dot_general(
        left, right, (((1,), (1,)), ((), ())), preferred_element_type=F32
    )


def local_stats(teach, learn, gap, axis):
    t_top = jnp.max(teach, axis=axis, keepdims=True)
    s_top = jnp.max(learn, axis=axis, keepdims=True)
    e = jnp.exp(teach - t_top)
    t_sum = jnp.sum(e, axis=axis)
    w = jnp.sum(e * gap, axis=axis)
    s_sum = jnp.sum(jnp.exp(learn - s_top), axis=axis)
    return jnp.stack([t_top.reshape(-1), t_sum, s_top.reshape(-1), s_sum, w])


def merge(parts):
    t_top = parts[0][0]
    s_top = parts[0][2]
    for p in parts[1:]:
        t_top = jnp.maximum(t_top, p[0])
        s_top = jnp.maximum(s_top, p[2])
    t_sum = s_sum = w = 0.0
    for p in parts:
        a = jnp.exp(p[0] - t_top)
        t_sum = t_sum + p[1] * a
        w = w + p[4] * a
        s_sum = s_sum + p[3] * jnp.exp(p[2] - s_top)
    return jnp.stack([t_top, t_sum, s_top, s_sum, w])


def merge_rows(st):
    for move, axis in ((move_x, 2), (move_y, 1)):
        st = merge([st] + [jnp.roll(move(st, s), -s, axis=axis) for s in (1, -1, 2)])
    return st


def merge_cols(st):
    flip = [(8 - j) % 8 for j in range(8)]
    st = merge([st, jnp.stack([move_c(st)[:, j] for j in flip], axis=1)[:, :, ::-1]])

    def from_ahead(v, d):
        return jnp.roll(move_z(v, d), d, axis=1)

    a = from_ahead(st, 1)
    b = from_ahead(st, -1)
    two = merge([st, a])
    three = merge([two, b])
    return merge([three, from_ahead(three, 3), from_ahead(two, -3)])


def reduce_rows(v, core):
    _, _, n, d = v.shape
    h = d // 2
    v = v.astype(BF).reshape(NY, NX, n, 2, h)
    by_half = v.transpose(3, 0, 1, 2, 4)
    keep = jnp.where(core == 0, by_half[0], by_half[1].transpose(1, 0, 2, 3))
    give = jnp.where(core == 0, by_half[1].transpose(1, 0, 2, 3), by_half[0])
    v = jnp.stack([keep, move_c(give)])
    far_a = move_first(v[0, :, 2], 1)
    far_b = move_first(v[1, :, 2], -1)
    up = v[:, :, 1].at[0].set((v[0, :, 1].astype(F32) + far_a.astype(F32)).astype(BF))
    down = v[:, :, 3].at[1].set((v[1, :, 3].astype(F32) + far_b.astype(F32)).astype(BF))
    r_up = move_first(up, 1)
    r_down = move_first(down, -1)
    v = v[:, :, 0].astype(F32) + r_up.astype(F32) + r_down.astype(F32)
    w = v.astype(BF)
    total = v[:, 0]
    for k, s in ((1, 1), (3, -1), (2, 2)):
        total = total + move_second(w[:, k], s).astype(F32)
    total = total.astype(BF)
    got = move_c(total[1])
    return jnp.where(
        core == 0,
        jnp.concatenate([total[0], got], axis=1),
        jnp.concatenate([got, total[0]], axis=1),
    )


def reduce_cols(v):
    n, d = v.shape[2:]
    give = jnp.concatenate(
        [v[0, 1:], v[4, 1:], v[1, ::-1], v[2, ::-1], v[3, ::-1]]
    ).astype(BF)
    got = move_c(give).astype(F32)
    k0 = v[0, 0] + got[0]
    k4 = v[4, 0] + got[1]
    k7 = v[7] + got[2:4]
    k6 = v[6] + got[4:6]
    k5 = v[5] + got[6:8]
    u = move_z(k4.astype(BF), 1).astype(F32)
    u = move_z(jnp.stack([k5[0] + u, k5[1]]).astype(BF), 1).astype(F32)
    u = move_z((k6 + u).astype(BF), 1).astype(F32)
    u = move_z((k7 + u).astype(BF), 1)
    return k0 + u[0].astype(F32) + move_c(u[1]).astype(F32)


def per_device(teacher_image, teacher_text, student_image, student_text):
    n, d = teacher_image.shape
    total_pairs = n * NX * NY * NZ * NC
    core = lax.axis_index("row") % 2
    keep = jnp.where(core == 0, teacher_image, student_image)
    give = jnp.where(core == 0, student_image, teacher_image)
    shared = move_c(jnp.stack([give, teacher_text, student_text]))
    t_cols, s_cols = gather_cols(jnp.stack([jnp.stack([teacher_text, student_text]), shared[1:]]))
    mine, got = gather_rows(jnp.stack([keep, shared[0]]))
    t_rows = jnp.where(core == 0, mine, got).reshape(-1, d)
    s_rows = jnp.where(core == 0, got, mine).transpose(1, 0, 2, 3).reshape(-1, d)
    teach = similarity(t_rows, t_cols)
    learn = similarity(s_rows, s_cols)
    gap = teach - learn
    row_st = local_stats(teach, learn, gap, 1).reshape(5, NY, NX, n)
    col_st = local_stats(teach, learn, gap, 0).reshape(5, NZ, NC, n)
    row_st = merge_rows(row_st).reshape(5, -1)
    col_st = merge_cols(col_st).reshape(5, -1)
    row_t = row_st[0] + jnp.log(row_st[1])
    row_s = row_st[2] + jnp.log(row_st[3])
    col_t = col_st[0] + jnp.log(col_st[1])
    col_s = col_st[2] + jnp.log(col_st[3])
    coupling = 0.5 * (
        jnp.exp(learn - row_s[:, None])
        - jnp.exp(teach - row_t[:, None])
        + jnp.exp(learn - col_s[None, :])
        - jnp.exp(teach - col_t[None, :])
    )
    coupling = coupling.astype(BF)
    text = 100.0 * lax.dot_general(
        coupling, s_rows, (((0,), (0,)), ((), ())), preferred_element_type=F32
    )
    text_grad = reduce_cols(text.reshape(NZ, NC, n, d))
    image = 100.0 * jnp.dot(coupling, s_cols, preferred_element_type=F32)
    image_grad = reduce_rows(image.reshape(NY, NX, n, d), core)
    part_r = jnp.sum(row_st[4] / row_st[1] + (row_s - row_t))
    part_c = jnp.sum(col_st[4] / col_st[1] + (col_s - col_t))
    part_r, part_c, _ = lax.optimization_barrier((part_r, part_c, coupling))
    lr = jnp.full((8, 128), part_r, F32)
    lr = lr + move_c(lr)
    for s in (1, 2, 4):
        lr = lr + move_z(lr, s)
    lc = jnp.full((8, 128), part_c, F32)
    for mv in (move_x, move_y):
        for s in (1, 2):
            lc = lc + mv(lc, s)
    loss = (lr[0, 0] + lc[0, 0]) * (0.5 / total_pairs)
    return (image_grad.astype(BF), text_grad.astype(BF), loss)


def solution(mesh):
    placed = P(("row", "col"), None)
    return jax.shard_map(
        per_device,
        mesh=mesh,
        in_specs=(placed,) * 4,
        out_specs=(placed, placed, P()),
        check_vma=False,
    )
```

```python
import jax
import jax.numpy as jnp
from jax import lax
from jax.experimental import pallas as pl
from jax.experimental.pallas import tpu as pltpu
from jax.sharding import PartitionSpec as P

NX, NY, NZ, NC = 4, 4, 8, 2
BF = jnp.bfloat16
F32 = jnp.float32
GROUP = 8
LANES = 128
VMEM_BYTES = 16 << 20
PASS_1_BYTES = 40 << 20
PASS_2_BYTES = 52 << 20


def place(z, c, y, x):
    return ((z % NZ * NC + c) * NY + y % NY) * NX + x % NX


def send(v, target):
    pairs = [
        (place(z, c, y, x), place(*target(z, c, y, x)))
        for z in range(NZ)
        for c in range(NC)
        for y in range(NY)
        for x in range(NX)
    ]
    return lax.ppermute(v, ("row", "col"), pairs)


def swap(v, z_bits=0, c_bits=0, y_bits=0, x_bits=0):
    return send(v, lambda z, c, y, x: (z ^ z_bits, c ^ c_bits, y ^ y_bits, x ^ x_bits))


def move_first(v, d):
    return send(v, lambda z, c, y, x: (z, c, y + d * c, x + d * (1 - c)))


def move_second(v, d):
    return send(v, lambda z, c, y, x: (z, c, y + d * (1 - c), x + d * c))


def move_z(v, d):
    return send(v, lambda z, c, y, x: (z + d * (1 - 2 * c), c, y, x))


def position():
    row, col = lax.axis_index("row"), lax.axis_index("col")
    return lax.div(row, NC), lax.rem(row, NC), lax.div(col, NX), lax.rem(col, NX)


def gather_rows(v):
    from_m = move_first(v, 1)
    from_p = move_first(v, -1)
    from_2 = move_first(v, 2)
    line = jnp.stack([v, from_p, from_2, from_m], axis=1)
    up = move_second(line, 1)
    down = move_second(line, -1)
    far_a = move_second(up[:, :2], 1)
    far_b = move_second(down[:, 2:], -1)
    got_0 = swap(line[1], c_bits=1)
    got_1 = swap(jnp.stack([down[1], up[1]]), c_bits=1)
    got_2 = swap(jnp.concatenate([far_a[1], far_b[1]]), c_bits=1)
    return line, up, down, far_a, far_b, got_0, got_1, got_2


def gather_cols(v):
    out = [v]
    for _ in range(3):
        out.append(move_z(out[-1], 1))
    far = move_z(out[3][0], 1)
    back = [swap(b, c_bits=1) for b in out[1:]]
    return out + [far] + back + [swap(far, c_bits=1)]


def pass_1_kernel(
    line, up, down, far_a, far_b, got_0, got_1, got_2,
    t0, t1, t2, t3, far, b1, b2, b3, far_sib,
    both_out, student, row_st, col_st,
    teach, learn, rows, cols, tops, wide, sums, sem,
):
    z, c, y, x = position()
    n, d = rows.shape[2:]
    size = teach.shape[0]
    tiles = size // LANES

    def row_place(second, first):
        dy = second * (1 - c) + first * c
        dx = first * (1 - c) + second * c
        return lax.rem(y + dy, NY) * NX + lax.rem(x + dx, NX)

    def col_place(steps, core):
        return lax.rem(z + NZ + steps, NZ) * NC + core

    pieces = []
    for k in range(4):
        for f in range(4):
            if k == 2:
                src = (far_a, (0, f)) if f < 2 else (far_b, (0, f - 2))
            else:
                src = ({0: line, 1: down, 3: up}[k], (0, f))
            pieces.append((src, (rows, c, row_place(k, f))))
            src = {0: (got_0, k), 1: (got_1, (0, k)), 2: (got_2, k), 3: (got_1, (1, k))}[f]
            pieces.append((src, (rows, 1 - c, row_place(k, f))))
    way = 2 * c - 1
    for kind in range(2):
        for j, ref in enumerate((t0, t1, t2, t3)):
            for dc in range(2):
                core = c if dc == 0 else 1 - c
                pieces.append(((ref, (dc, kind)), (cols, kind, col_place(way * j, core))))
        for j, ref in enumerate((b1, b2, b3)):
            for dc in range(2):
                core = 1 - c if dc == 0 else c
                pieces.append(((ref, (dc, kind)), (cols, kind, col_place(-way * (j + 1), core))))
        pieces.append(((far, kind), (cols, kind, col_place(4, c))))
        pieces.append(((far_sib, kind), (cols, kind, col_place(4, 1 - c))))
    for (src, i), (dst, j, k) in pieces:
        dst[j, k] = src[i]
    leave = [
        pltpu.make_async_copy(rows.at[1], student.at[0], sem.at[0]),
        pltpu.make_async_copy(cols.at[1], student.at[1], sem.at[1]),
    ]
    for copy in leave:
        copy.start()

    for kind, buf in ((0, teach), (1, learn)):
        buf[...] = 100.0 * lax.dot_general(
            rows[kind].reshape(size, d),
            cols[kind].reshape(size, d),
            (((1,), (1,)), ((), ())),
            preferred_element_type=F32,
        )
        copy = pltpu.make_async_copy(buf, both_out.at[kind], sem.at[2 + kind])
        copy.start()
        leave.append(copy)

    def tile(ref, part, q):
        return ref[part, q * LANES : (q + 1) * LANES]

    def top_step(i, carry):
        part = pl.ds(pl.multiple_of(i * GROUP, GROUP), GROUP)
        out = []
        for k, ref in ((0, teach), (1, learn)):
            v = [tile(ref, part, q) for q in range(tiles)]
            out.append([jnp.maximum(a, b) for a, b in zip(carry[k], v)])
            while len(v) > 1:
                v = [jnp.maximum(a, b) for a, b in zip(v[::2], v[1::2])]
            tops[k, part, :] = v[0]
        return out

    low = jnp.full((GROUP, LANES), -jnp.inf, F32)
    col_tops = lax.fori_loop(0, size // GROUP, top_step, [[low] * tiles] * 2, unroll=2)
    col_tops = [[jnp.max(v, axis=0, keepdims=True) for v in tops_k] for tops_k in col_tops]
    row_tops = []
    for k in range(2):
        top = jnp.max(tops[k].T, axis=0, keepdims=True)
        row_tops.append(top)
        wide[k] = jnp.broadcast_to(top, (LANES, size)).T

    for h in range(2):
        span = range(h * tiles // 2, (h + 1) * tiles // 2)
        t_tops = [jnp.broadcast_to(col_tops[0][q], (GROUP, LANES)) for q in span]
        s_tops = [jnp.broadcast_to(col_tops[1][q], (GROUP, LANES)) for q in span]

        def sum_step(i, carry):
            part = pl.ds(pl.multiple_of(i * GROUP, GROUP), GROUP)
            rt, rs = wide[0, part, :], wide[1, part, :]
            acc = [0.0, 0.0, 0.0] if h == 0 else [sums[k, part, :] for k in range(3)]
            out = []
            for j, q in enumerate(span):
                t, s = tile(teach, part, q), tile(learn, part, q)
                gap = t - s
                e = jnp.exp(t - rt)
                acc = [acc[0] + e, acc[1] + jnp.exp(s - rs), acc[2] + e * gap]
                e = jnp.exp(t - t_tops[j])
                a, b, w = carry[j]
                out.append((a + e, b + jnp.exp(s - s_tops[j]), w + e * gap))
            for k in range(3):
                sums[k, part, :] = acc[k]
            return out

        none = jnp.zeros((GROUP, LANES), F32)
        out = lax.fori_loop(0, size // GROUP, sum_step, [(none,) * 3] * len(span), unroll=2)
        for j, q in enumerate(span):
            a, b, w = [jnp.sum(v, axis=0, keepdims=True) for v in out[j]]
            zero = jnp.zeros_like(w)
            col_st[:, q * LANES : (q + 1) * LANES] = jnp.concatenate(
                [col_tops[0][q], a, col_tops[1][q], b, w, zero, zero, zero], axis=0
            )
    a, b, w = [jnp.sum(sums[k].T, axis=0, keepdims=True) for k in range(3)]
    zero = jnp.zeros_like(w)
    row_st[...] = jnp.concatenate([row_tops[0], a, row_tops[1], b, w, zero, zero, zero], axis=0)
    for copy in leave:
        copy.wait()


def pass_1(pieces, n, d):
    size = NY * NX * n
    vmem = pl.BlockSpec(memory_space=pltpu.VMEM)
    hbm = pl.BlockSpec(memory_space=pltpu.HBM)
    both = jax.ShapeDtypeStruct((2, size, size), F32)
    blocks = jax.ShapeDtypeStruct((2, 16, n, d), BF)
    small = jax.ShapeDtypeStruct((8, size), F32)
    return pl.pallas_call(
        pass_1_kernel,
        out_shape=(both, blocks, small, small),
        in_specs=[vmem] * len(pieces),
        out_specs=(hbm, hbm, vmem, vmem),
        scratch_shapes=[
            pltpu.VMEM((size, size), F32),
            pltpu.VMEM((size, size), F32),
            pltpu.VMEM((2, 16, n, d), BF),
            pltpu.VMEM((2, 16, n, d), BF),
            pltpu.VMEM((2, size, LANES), F32),
            pltpu.VMEM((2, size, LANES), F32),
            pltpu.VMEM((3, size, LANES), F32),
            pltpu.SemaphoreType.DMA((4,)),
        ],
        compiler_params=pltpu.CompilerParams(vmem_limit_bytes=PASS_1_BYTES),
        cost_estimate=pl.CostEstimate(
            flops=4 * size * size * d, bytes_accessed=20 << 20, transcendentals=4 * size * size
        ),
    )(*pieces)


def merge(parts):
    parts = [[p[k : k + 1] for k in range(5)] for p in parts]
    t_top = parts[0][0]
    s_top = parts[0][2]
    for p in parts[1:]:
        t_top = jnp.maximum(t_top, p[0])
        s_top = jnp.maximum(s_top, p[2])
    terms = []
    for p in parts:
        a = jnp.exp(p[0] - t_top)
        terms.append((p[1] * a, p[3] * jnp.exp(p[2] - s_top), p[4] * a))
    while len(terms) > 1:
        terms = [
            tuple(u + v for u, v in zip(terms[i], terms[i + 1])) for i in range(0, len(terms), 2)
        ]
    t_sum, s_sum, w = terms[0]
    return [t_top, t_sum, s_top, s_sum, w]


def merged(parts):
    return jnp.concatenate(merge(parts), axis=0)


def pass_2_kernel(
    both_in, student_in, ra, rb, rc, rd, ca, cb,
    give, keep_image, keep_text, loss_part,
    teach, learn, rows, cols, coupling, wide, product, sem,
):
    z, c, y, x = position()
    n, d = rows.shape[1:]
    size = teach.shape[0]
    half = d // 2
    chunk = size // 4
    enter = []
    for r in range(4):
        part = pl.ds(r * chunk, chunk)
        for k, dst in ((0, teach), (1, learn)):
            enter.append(pltpu.make_async_copy(both_in.at[k, part], dst.at[part], sem.at[len(enter)]))
    enter.append(pltpu.make_async_copy(student_in.at[0], rows, sem.at[8]))
    enter.append(pltpu.make_async_copy(student_in.at[1], cols, sem.at[9]))
    for copy in enter:
        copy.start()
    row_st = merge([r[...] for r in (ra, rb, rc, rd)])
    col_st = merge([r[...] for r in (ca, cb)])
    row_t, row_s = row_st[0] + jnp.log(row_st[1]), row_st[2] + jnp.log(row_st[3])
    col_t, col_s = col_st[0] + jnp.log(col_st[1]), col_st[2] + jnp.log(col_st[3])
    part_r = jnp.sum(row_st[4] / row_st[1] + (row_s - row_t), axis=1, keepdims=True)
    part_c = jnp.sum(col_st[4] / col_st[1] + (col_s - col_t), axis=1, keepdims=True)
    loss_part[0] = jnp.broadcast_to(part_r, (8, LANES))
    loss_part[1] = jnp.broadcast_to(part_c, (8, LANES))
    whole = jnp.broadcast_to(part_r, (16, half))
    for k in range(3):
        piece = whole.astype(BF)
        give[32, 16 * k : 16 * k + 16] = piece
        whole = whole - piece.astype(F32)
    give[32, 48:] = jnp.zeros((n - 48, half), BF)
    for k, v in ((0, row_t), (1, row_s)):
        wide[k] = jnp.broadcast_to(v, (LANES, size)).T

    span = 4

    def chunk_step(r, carry):
        part = pl.ds(pl.multiple_of(r * chunk, chunk), chunk)
        pltpu.make_async_copy(both_in.at[0, part], teach.at[part], sem.at[2 * r]).wait()
        pltpu.make_async_copy(both_in.at[1, part], learn.at[part], sem.at[2 * r + 1]).wait()
        for h in range(size // (span * LANES)):
            lanes = [slice((h * span + j) * LANES, (h * span + j + 1) * LANES) for j in range(span)]
            ct = [jnp.broadcast_to(col_t[:, s], (16, LANES)) for s in lanes]
            cs = [jnp.broadcast_to(col_s[:, s], (16, LANES)) for s in lanes]

            def step(i, inner):
                part = pl.ds(pl.multiple_of(i * 16, 16), 16)
                rt, rs = wide[0, part, :], wide[1, part, :]
                for j in range(span):
                    t, s = teach[part, lanes[j]], learn[part, lanes[j]]
                    v = jnp.exp(s - rs) - jnp.exp(t - rt) + jnp.exp(s - cs[j]) - jnp.exp(t - ct[j])
                    coupling[part, lanes[j]] = (0.5 * v).astype(BF)
                return inner

            lax.fori_loop(r * (chunk // 16), (r + 1) * (chunk // 16), step, 0)
        return carry

    lax.fori_loop(0, 4, chunk_step, 0)
    enter[8].wait()
    enter[9].wait()

    def text_step(i, carry):
        part = pl.ds(pl.multiple_of(i * chunk, chunk), chunk)
        product[part, :] = 100.0 * lax.dot_general(
            coupling[:, part],
            rows[...].reshape(size, d),
            (((0,), (0,)), ((), ())),
            preferred_element_type=F32,
        )
        return carry

    lax.fori_loop(0, 4, text_step, 0)
    out = 1 - 2 * c

    def text_block(k, core):
        at = lax.rem(z + NZ + k, NZ) * NC + core
        return product[pl.ds(pl.multiple_of(at * n, n), n), :]

    def put(i, v):
        v = v.astype(BF)
        give[16 + i] = v[:, :half]
        give[24 + i] = v[:, half:]

    put(0, text_block(0, 1 - c))
    put(1, text_block(4, 1 - c))
    keep_text[0] = text_block(0, c)
    keep_text[1] = text_block(4, c)
    for k in (1, 2, 3):
        for core in range(2):
            put(2 * k + core, text_block(-out * k, core))
            keep_text[2 * k + core] = text_block(out * k, core)

    def image_step(i, carry):
        lanes = pl.ds(pl.multiple_of(i * (d // 4), d // 4), d // 4)
        product[:, lanes] = 100.0 * jnp.dot(
            coupling[...], cols[:, :, lanes].reshape(size, d // 4), preferred_element_type=F32
        )
        return carry

    lax.fori_loop(0, 4, image_step, 0)
    mine = pl.ds(pl.multiple_of(c * half, half), half)
    other = pl.ds(pl.multiple_of((1 - c) * half, half), half)
    for k in range(4):
        for f in range(4):
            dy = k * (1 - c) + f * c
            dx = f * (1 - c) + k * c
            at = lax.rem(y + dy, NY) * NX + lax.rem(x + dx, NX)
            part = pl.ds(pl.multiple_of(at * n, n), n)
            keep_image[f * 4 + k] = product[part, mine].astype(BF)
            give[k * 4 + f] = product[part, other].astype(BF)


def pass_2(args, n, d):
    size = NY * NX * n
    vmem = pl.BlockSpec(memory_space=pltpu.VMEM)
    return pl.pallas_call(
        pass_2_kernel,
        out_shape=(
            jax.ShapeDtypeStruct((33, n, d // 2), BF),
            jax.ShapeDtypeStruct((16, n, d // 2), BF),
            jax.ShapeDtypeStruct((8, n, d), F32),
            jax.ShapeDtypeStruct((2, 8, LANES), F32),
        ),
        in_specs=[pl.BlockSpec(memory_space=pltpu.HBM)] * 2 + [vmem] * (len(args) - 2),
        out_specs=(vmem,) * 4,
        scratch_shapes=[
            pltpu.VMEM((size, size), F32),
            pltpu.VMEM((size, size), F32),
            pltpu.VMEM((16, n, d), BF),
            pltpu.VMEM((16, n, d), BF),
            pltpu.VMEM((size, size), BF),
            pltpu.VMEM((2, size, LANES), F32),
            pltpu.VMEM((size, d), F32),
            pltpu.SemaphoreType.DMA((10,)),
        ],
        compiler_params=pltpu.CompilerParams(vmem_limit_bytes=PASS_2_BYTES),
        cost_estimate=pl.CostEstimate(
            flops=4 * size * size * d, bytes_accessed=20 << 20, transcendentals=4 * size * size
        ),
    )(*args)


def vmem_call(kernel, outs, args):
    vmem = pl.BlockSpec(memory_space=pltpu.VMEM)
    return pl.pallas_call(
        kernel,
        out_shape=tuple(jax.ShapeDtypeStruct(s, t) for s, t in outs),
        in_specs=[vmem] * len(args),
        out_specs=(vmem,) * len(outs),
        compiler_params=pltpu.CompilerParams(vmem_limit_bytes=VMEM_BYTES),
        cost_estimate=pl.CostEstimate(flops=1 << 20, bytes_accessed=4 << 20, transcendentals=0),
    )(*args)


def pack(ref, row, lane, v):
    v = jnp.broadcast_to(v, (16, LANES))
    for k in range(3):
        piece = v.astype(BF)
        ref[row : row + 16, lane + k * LANES : lane + (k + 1) * LANES] = piece
        v = v - piece.astype(F32)


def unpack(ref, row, lane):
    v = ref[row : row + 16, lane : lane + 3 * LANES].astype(F32)
    return (v[:1, :LANES] + v[:1, LANES : 2 * LANES]) + v[:1, 2 * LANES :]


def choose(flag, a, b):
    return jnp.where(flag + jnp.zeros(a.shape, jnp.int32) == 0, a, b)


def load_kernel(
    keep_text, keep_image, got, loss_part,
    text_own, k1, k2, k34, image_own, p1, m1, far, rows_loss,
):
    z, _, _, _ = position()
    n, h = got.shape[1:]
    for i in range(8):
        for q in range(2):
            lanes = slice(q * h, (q + 1) * h)
            v = keep_text[i, :, lanes] + got[16 + 8 * q + i].astype(F32)
            if i == 0:
                text_own[:, lanes] = v
            elif i == 1:
                k34[2 * n : 3 * n, lanes] = v.astype(BF)
            elif i >= 6:
                k34[(i - 6) * n : (i - 5) * n, lanes] = v.astype(BF)
            else:
                (k1, k2)[i // 2 - 1][i % 2, :, lanes] = v
    image_own[0] = keep_image[0:4]
    image_own[1] = got[0:4]
    cols_loss = loss_part[1, :1]
    for f, out in ((1, p1), (2, far), (3, m1)):
        out[: 4 * n] = keep_image[f * 4 : f * 4 + 4].reshape(4 * n, h)
        out[4 * n : 8 * n] = got[f * 4 : f * 4 + 4].reshape(4 * n, h)
        out[8 * n :] = jnp.zeros((16, h), BF)
        pack(out, 8 * n, 0, cols_loss)
    sib = got[32].astype(F32)
    chip = loss_part[0, :1] + ((sib[0:1, :LANES] + sib[16:17, :LANES]) + sib[32:33, :LANES])
    lane = lax.broadcasted_iota(jnp.int32, (1, LANES), 1)
    mine = jnp.where(lane == z, chip, 0.0)
    rows_loss[...] = jnp.broadcast_to(mine, (8, LANES))
    k34[3 * n :] = jnp.zeros((16, 2 * h), BF)
    pack(k34, 3 * n, 0, mine)


def pass_on_kernel(k1, k2, k34, rows_loss, b1, b2):
    _, c, _, _ = position()
    n, d = k1.shape[1:]
    for core in range(2):
        part = slice(core * n, (core + 1) * n)
        b1[part] = (k1[core] + k34[part].astype(F32)).astype(BF)
        v = k34[2 * n : 3 * n].astype(F32)
        b2[part] = (k2[core] + choose(c - core, v, jnp.zeros_like(v))).astype(BF)
    came = unpack(k34, 3 * n, 0)
    for ref in (b1, b2):
        ref[2 * n :] = jnp.zeros((16, d), BF)
    pack(b1, 2 * n, 0, rows_loss[:1] + came)
    pack(b2, 2 * n, 0, came)


def ring_sum(odd, own, back, ahead, far):
    return (own + choose(odd, ahead, back)) + (far + choose(odd, back, ahead))


def line_kernel(own, p1, m1, far, loss_part, out, w1, w2, w3, cols_loss):
    _, c, y, x = position()
    n, h = own.shape[2:]
    for k, ref in enumerate((out, w1, w2, w3)):
        for core in range(2):
            part = slice((core * 4 + k) * n, (core * 4 + k + 1) * n)
            v = own[core, k].astype(F32) + far[part].astype(F32)
            v = v + p1[part].astype(F32) + m1[part].astype(F32)
            ref[core * n : (core + 1) * n] = v.astype(ref.dtype)
    odd = lax.rem(x * (1 - c) + y * c, 2)
    v = ring_sum(odd, loss_part[1, :1], *[unpack(r, 8 * n, 0) for r in (p1, m1, far)])
    cols_loss[...] = jnp.broadcast_to(v, (8, LANES))
    for ref in (w1, w2, w3):
        ref[2 * n :] = jnp.zeros((16, h), BF)
        pack(ref, 2 * n, 0, v)


def last_kernel(
    text_own, b1, b2, k34, rows_loss, line, w1, w2, w3, cols_loss,
    text, image, share, loss,
):
    _, c, y, x = position()
    n, d = text.shape
    ways = []
    for core in range(2):
        part = slice(core * n, (core + 1) * n)
        ways.append(b1[part].astype(F32) + b2[part].astype(F32))
    text[...] = text_own[...] + choose(c, ways[0], ways[1])
    share[:n, :d] = choose(c, ways[1], ways[0]).astype(BF)
    v = line[...]
    for r in (w1, w2, w3):
        v = v + r[: 2 * n].astype(F32)
    image[...] = v[:n].astype(BF)
    share[:n, d:] = v[n:].astype(BF)
    odd = lax.rem(y * (1 - c) + x * c, 2)
    cols = ring_sum(odd, cols_loss[:1], *[unpack(r, 2 * n, 0) for r in (w1, w3, w2)])
    near = unpack(k34, 3 * n, 0) + unpack(b1, 2 * n, 0)
    rows = choose(c, near + (rows_loss[:1] + unpack(b2, 2 * n, 0)), near)
    share[n:] = jnp.zeros((16, share.shape[1]), BF)
    pack(share, n, 0, rows)
    pack(share, n, 3 * LANES, cols)
    loss[0] = jnp.broadcast_to(rows, (8, LANES))
    loss[1] = jnp.broadcast_to(cols, (8, LANES))


def end_kernel(text, image, share, loss, text_grad, image_grad, total):
    _, c, _, _ = position()
    n, d = text.shape
    h = d // 2
    text_grad[...] = (text[...] + share[:n, :d].astype(F32)).astype(BF)
    mine, other = image[...].astype(F32), share[:n, d:].astype(F32)
    image_grad[:, :h] = choose(c, mine, other).astype(BF)
    image_grad[:, h:] = choose(c, other, mine).astype(BF)
    rows = loss[0, :1] + unpack(share, n, 0)
    cols = choose(c, loss[1, :1], unpack(share, n, 3 * LANES))
    total[...] = jnp.broadcast_to(jnp.sum(rows, axis=1, keepdims=True) + cols, (8, LANES))


def reduce_all(give, keep_image, keep_text, loss_part):
    n, d = keep_text.shape[1:]
    h = d // 2
    got = swap(give, c_bits=1)
    small = ((8, LANES), F32)
    pair, line_out = ((2, n, d), F32), ((8 * n + 16, h), BF)
    text_own, k1, k2, k34, image_own, p1, m1, far, rows_loss = vmem_call(
        load_kernel,
        [((n, d), F32), pair, pair, ((3 * n + 16, d), BF), ((2, 4, n, h), BF)]
        + [line_out] * 3
        + [small],
        (keep_text, keep_image, got, loss_part),
    )
    far = move_first(far, 2)
    k34 = move_z(k34, 2)
    p1 = move_first(p1, 1)
    m1 = move_first(m1, -1)
    b1, b2 = vmem_call(
        pass_on_kernel, [((2 * n + 16, d), BF)] * 2, (k1, k2, k34, rows_loss)
    )
    b1 = move_z(b1, 1)
    b2 = move_z(b2, 2)
    line, w1, w2, w3, cols_loss = vmem_call(
        line_kernel,
        [((2 * n, h), F32)] + [((2 * n + 16, h), BF)] * 3 + [small],
        (image_own, p1, m1, far, loss_part),
    )
    w1 = move_second(w1, 1)
    w2 = move_second(w2, 2)
    w3 = move_second(w3, -1)
    text, image, share, loss = vmem_call(
        last_kernel,
        [((n, d), F32), ((n, h), BF), ((n + 16, d + h), BF), ((2, 8, LANES), F32)],
        (text_own, b1, b2, k34, rows_loss, line, w1, w2, w3, cols_loss),
    )
    return vmem_call(
        end_kernel,
        [((n, d), BF), ((n, d), BF), small],
        (text, image, swap(share, c_bits=1), loss),
    )


def merge_steps(row_st, col_st):
    row_st = merged([row_st] + [swap(row_st, x_bits=b) for b in (1, 2, 3)])
    col_st = merged([col_st, swap(col_st, c_bits=1)])
    col_st = merged([col_st] + [swap(col_st, z_bits=b) for b in (1, 2, 3)])
    return [row_st] + [swap(row_st, y_bits=b) for b in (1, 2, 3)] + [
        col_st,
        swap(col_st, z_bits=4),
    ]


def per_device(teacher_image, teacher_text, student_image, student_text):
    n, d = teacher_image.shape
    total_pairs = n * NX * NY * NZ * NC
    core = lax.rem(lax.axis_index("row"), NC)
    keep = jnp.where(core == 0, teacher_image, student_image)
    give = jnp.where(core == 0, student_image, teacher_image)
    shared = swap(jnp.stack([give, teacher_text, student_text]), c_bits=1)
    text_blocks = gather_cols(
        jnp.stack([jnp.stack([teacher_text, student_text]), shared[1:]])
    )
    image_blocks = gather_rows(jnp.stack([keep, shared[0]]))
    both, student, row_st, col_st = pass_1(
        list(image_blocks) + list(text_blocks), n, d
    )
    give, keep_image, keep_text, loss_part = pass_2(
        [both, student] + merge_steps(row_st, col_st), n, d
    )
    text_grad, image_grad, loss = reduce_all(give, keep_image, keep_text, loss_part)
    return (image_grad, text_grad, loss[0, 0] * (0.5 / total_pairs))


def solution(mesh):
    placed = P(("row", "col"), None)
    return jax.shard_map(
        per_device,
        mesh=mesh,
        in_specs=(placed,) * 4,
        out_specs=(placed, placed, P()),
        check_vma=False,
    )
```

```python
import functools

import jax
import jax.numpy as jnp
from jax import lax
from jax.experimental import pallas as pl
from jax.experimental.pallas import tpu as pltpu
from jax.sharding import PartitionSpec as P

NX, NY, NZ, NC = 4, 4, 8, 2
BF = jnp.bfloat16
F32 = jnp.float32
GROUP = 8
LANES = 128
VMEM_BYTES = 16 << 20
PASS_1_BYTES = 40 << 20
PASS_2_BYTES = 48 << 20


def place(z, c, y, x):
    return ((z % NZ * NC + c) * NY + y % NY) * NX + x % NX


def send(v, target):
    pairs = [
        (place(z, c, y, x), place(*target(z, c, y, x)))
        for z in range(NZ)
        for c in range(NC)
        for y in range(NY)
        for x in range(NX)
    ]
    return lax.ppermute(v, ("row", "col"), pairs)


def swap(v, z_bits=0, c_bits=0, y_bits=0, x_bits=0):
    return send(v, lambda z, c, y, x: (z ^ z_bits, c ^ c_bits, y ^ y_bits, x ^ x_bits))


def move_first(v, d):
    return send(v, lambda z, c, y, x: (z, c, y + d * c, x + d * (1 - c)))


def move_second(v, d):
    return send(v, lambda z, c, y, x: (z, c, y + d * (1 - c), x + d * c))


def move_z(v, d):
    return send(v, lambda z, c, y, x: (z + d * (1 - 2 * c), c, y, x))


def position():
    row, col = lax.axis_index("row"), lax.axis_index("col")
    return lax.div(row, NC), lax.rem(row, NC), lax.div(col, NX), lax.rem(col, NX)


def gather_rows(v):
    from_m = move_first(v, 1)
    from_p = move_first(v, -1)
    from_2 = move_first(v, 2)
    line = jnp.stack([v, from_p, from_2, from_m], axis=1)
    up = move_second(line, 1)
    down = move_second(line, -1)
    far_a = move_second(up[:, :2], 1)
    far_b = move_second(down[:, 2:], -1)
    got_1 = swap(jnp.stack([line[1], down[1], up[1]]), c_bits=1)
    got_2 = swap(jnp.concatenate([far_a[1], far_b[1]]), c_bits=1)
    return line, up, down, far_a, far_b, got_1, got_2


def gather_cols(v):
    out = [v]
    for _ in range(3):
        out.append(move_z(out[-1], 1))
    far = move_z(out[3][0], 1)
    back = swap(jnp.stack(out[1:3]), c_bits=1)
    return out + [far, back, swap(out[3], c_bits=1), swap(far, c_bits=1)]


def pass_1_kernel(
    line, up, down, far_a, far_b, got_1, got_2,
    t0, t1, t2, t3, far, back, b3, far_sib,
    both_out, student, row_st, col_st,
    teach, learn, rows, cols, tops, wide, sums, sem,
):
    z, c, y, x = position()
    n, d = rows.shape[2:]
    size = teach.shape[0]
    tiles = size // LANES

    def row_place(second, first):
        dy = second * (1 - c) + first * c
        dx = first * (1 - c) + second * c
        return lax.rem(y + dy, NY) * NX + lax.rem(x + dx, NX)

    def col_place(steps, core):
        return lax.rem(z + NZ + steps, NZ) * NC + core

    pieces = []
    for k in range(4):
        for f in range(4):
            if k == 2:
                src = (far_a, (0, f)) if f < 2 else (far_b, (0, f - 2))
            else:
                src = ({0: line, 1: down, 3: up}[k], (0, f))
            pieces.append((src, (rows, c, row_place(k, f))))
            src = {0: (got_1, (0, k)), 1: (got_1, (1, k)), 2: (got_2, k), 3: (got_1, (2, k))}[f]
            pieces.append((src, (rows, 1 - c, row_place(k, f))))
    way = 2 * c - 1
    for kind in range(2):
        for j, ref in enumerate((t0, t1, t2, t3)):
            for dc in range(2):
                core = c if dc == 0 else 1 - c
                pieces.append(((ref, (dc, kind)), (cols, kind, col_place(way * j, core))))
        for j in range(3):
            for dc in range(2):
                core = 1 - c if dc == 0 else c
                src = (back, (j, dc, kind)) if j < 2 else (b3, (dc, kind))
                pieces.append((src, (cols, kind, col_place(-way * (j + 1), core))))
        pieces.append(((far, kind), (cols, kind, col_place(4, c))))
        pieces.append(((far_sib, kind), (cols, kind, col_place(4, 1 - c))))
    for (src, i), (dst, j, k) in pieces:
        dst[j, k] = src[i]
    leave = [
        pltpu.make_async_copy(rows.at[1], student.at[0], sem.at[0]),
        pltpu.make_async_copy(cols.at[1], student.at[1], sem.at[1]),
    ]
    for copy in leave:
        copy.start()

    for kind, buf in ((0, teach), (1, learn)):
        buf[...] = 100.0 * lax.dot_general(
            rows[kind].reshape(size, d),
            cols[kind].reshape(size, d),
            (((1,), (1,)), ((), ())),
            preferred_element_type=F32,
        )
        copy = pltpu.make_async_copy(buf, both_out.at[kind], sem.at[2 + kind])
        copy.start()
        leave.append(copy)

    def tile(ref, part, q):
        return ref[part, q * LANES : (q + 1) * LANES]

    def top_step(i, carry):
        part = pl.ds(pl.multiple_of(i * GROUP, GROUP), GROUP)
        out = []
        for k, ref in ((0, teach), (1, learn)):
            v = [tile(ref, part, q) for q in range(tiles)]
            out.append([jnp.maximum(a, b) for a, b in zip(carry[k], v)])
            while len(v) > 1:
                v = [jnp.maximum(a, b) for a, b in zip(v[::2], v[1::2])]
            tops[k, part, :] = v[0]
        return out

    low = jnp.full((GROUP, LANES), -jnp.inf, F32)
    col_tops = lax.fori_loop(0, size // GROUP, top_step, [[low] * tiles] * 2, unroll=2)
    col_tops = [[jnp.max(v, axis=0, keepdims=True) for v in tops_k] for tops_k in col_tops]
    row_tops = []
    for k in range(2):
        top = jnp.max(tops[k].T, axis=0, keepdims=True)
        row_tops.append(top)
        wide[k] = jnp.broadcast_to(top, (LANES, size)).T

    for h in range(2):
        span = range(h * tiles // 2, (h + 1) * tiles // 2)
        t_tops = [jnp.broadcast_to(col_tops[0][q], (GROUP, LANES)) for q in span]
        s_tops = [jnp.broadcast_to(col_tops[1][q], (GROUP, LANES)) for q in span]

        def sum_step(i, carry):
            part = pl.ds(pl.multiple_of(i * GROUP, GROUP), GROUP)
            rt, rs = wide[0, part, :], wide[1, part, :]
            acc = [0.0, 0.0, 0.0] if h == 0 else [sums[k, part, :] for k in range(3)]
            out = []
            for j, q in enumerate(span):
                t, s = tile(teach, part, q), tile(learn, part, q)
                gap = t - s
                e = jnp.exp(t - rt)
                acc = [acc[0] + e, acc[1] + jnp.exp(s - rs), acc[2] + e * gap]
                e = jnp.exp(t - t_tops[j])
                a, b, w = carry[j]
                out.append((a + e, b + jnp.exp(s - s_tops[j]), w + e * gap))
            for k in range(3):
                sums[k, part, :] = acc[k]
            return out

        none = jnp.zeros((GROUP, LANES), F32)
        out = lax.fori_loop(0, size // GROUP, sum_step, [(none,) * 3] * len(span), unroll=2)
        for j, q in enumerate(span):
            a, b, w = [jnp.sum(v, axis=0, keepdims=True) for v in out[j]]
            zero = jnp.zeros_like(w)
            col_st[:, q * LANES : (q + 1) * LANES] = jnp.concatenate(
                [col_tops[0][q], a, col_tops[1][q], b, w, zero, zero, zero], axis=0
            )
    a, b, w = [jnp.sum(sums[k].T, axis=0, keepdims=True) for k in range(3)]
    zero = jnp.zeros_like(w)
    row_st[...] = jnp.concatenate([row_tops[0], a, row_tops[1], b, w, zero, zero, zero], axis=0)
    for copy in leave:
        copy.wait()


def pass_1(pieces, n, d):
    size = NY * NX * n
    vmem = pl.BlockSpec(memory_space=pltpu.VMEM)
    hbm = pl.BlockSpec(memory_space=pltpu.HBM)
    both = jax.ShapeDtypeStruct((2, size, size), F32)
    blocks = jax.ShapeDtypeStruct((2, 16, n, d), BF)
    small = jax.ShapeDtypeStruct((8, size), F32)
    return pl.pallas_call(
        pass_1_kernel,
        out_shape=(both, blocks, small, small),
        in_specs=[vmem] * len(pieces),
        out_specs=(hbm, hbm, vmem, vmem),
        scratch_shapes=[
            pltpu.VMEM((size, size), F32),
            pltpu.VMEM((size, size), F32),
            pltpu.VMEM((2, 16, n, d), BF),
            pltpu.VMEM((2, 16, n, d), BF),
            pltpu.VMEM((2, size, LANES), F32),
            pltpu.VMEM((2, size, LANES), F32),
            pltpu.VMEM((3, size, LANES), F32),
            pltpu.SemaphoreType.DMA((4,)),
        ],
        compiler_params=pltpu.CompilerParams(vmem_limit_bytes=PASS_1_BYTES),
        cost_estimate=pl.CostEstimate(
            flops=4 * size * size * d, bytes_accessed=20 << 20, transcendentals=4 * size * size
        ),
    )(*pieces)


def merge(parts):
    parts = [[p[k : k + 1] for k in range(5)] for p in parts]
    t_top = parts[0][0]
    s_top = parts[0][2]
    for p in parts[1:]:
        t_top = jnp.maximum(t_top, p[0])
        s_top = jnp.maximum(s_top, p[2])
    terms = []
    for p in parts:
        a = jnp.exp(p[0] - t_top)
        terms.append((p[1] * a, p[3] * jnp.exp(p[2] - s_top), p[4] * a))
    while len(terms) > 1:
        terms = [
            tuple(u + v for u, v in zip(terms[i], terms[i + 1])) for i in range(0, len(terms), 2)
        ]
    t_sum, s_sum, w = terms[0]
    return [t_top, t_sum, s_top, s_sum, w]


def merged(parts):
    return jnp.concatenate(merge(parts), axis=0)


def pass_2_kernel(
    both_in, student_in, ra, rb, rc, rd, ca, cb,
    give, keep_image, keep_text, loss_part,
    teach, learn, rows, cols, coupling, wide, product, sem,
):
    z, c, y, x = position()
    n, d = rows.shape[1:]
    size = teach.shape[0]
    half = d // 2
    chunk = size // 4
    enter = []
    for r in range(4):
        part = pl.ds(r * chunk, chunk)
        for k, dst in ((0, teach), (1, learn)):
            enter.append(pltpu.make_async_copy(both_in.at[k, part], dst.at[part], sem.at[len(enter)]))
    enter.append(pltpu.make_async_copy(student_in.at[0], rows, sem.at[8]))
    enter.append(pltpu.make_async_copy(student_in.at[1], cols, sem.at[9]))
    for i in (0, 1, 9, 2, 3, 4, 5, 6, 7, 8):
        enter[i].start()
    row_st = merge([r[...] for r in (ra, rb, rc, rd)])
    col_st = merge([r[...] for r in (ca, cb)])
    row_t, row_s = row_st[0] + jnp.log(row_st[1]), row_st[2] + jnp.log(row_st[3])
    col_t, col_s = col_st[0] + jnp.log(col_st[1]), col_st[2] + jnp.log(col_st[3])
    part_r = jnp.sum(row_st[4] / row_st[1] + (row_s - row_t), axis=1, keepdims=True)
    part_c = jnp.sum(col_st[4] / col_st[1] + (col_s - col_t), axis=1, keepdims=True)
    loss_part[0] = jnp.broadcast_to(part_r, (8, LANES))
    loss_part[1] = jnp.broadcast_to(part_c, (8, LANES))
    whole = jnp.broadcast_to(part_r, (16, half))
    for k in range(3):
        piece = whole.astype(BF)
        give[32, 16 * k : 16 * k + 16] = piece
        whole = whole - piece.astype(F32)
    give[32, 48:] = jnp.zeros((n - 48, half), BF)
    for k, v in ((0, row_t), (1, row_s)):
        wide[k] = jnp.broadcast_to(v, (LANES, size)).T

    span = 4
    mine = pl.ds(pl.multiple_of(c * half, half), half)
    other = pl.ds(pl.multiple_of((1 - c) * half, half), half)

    def chunk_step(r, carry):
        part = pl.ds(pl.multiple_of(r * chunk, chunk), chunk)
        pltpu.make_async_copy(both_in.at[0, part], teach.at[part], sem.at[2 * r]).wait()
        pltpu.make_async_copy(both_in.at[1, part], learn.at[part], sem.at[2 * r + 1]).wait()
        for h in range(size // (span * LANES)):
            lanes = [slice((h * span + j) * LANES, (h * span + j + 1) * LANES) for j in range(span)]
            ct = [jnp.broadcast_to(col_t[:, s], (16, LANES)) for s in lanes]
            cs = [jnp.broadcast_to(col_s[:, s], (16, LANES)) for s in lanes]

            def step(i, inner):
                part = pl.ds(pl.multiple_of(i * 16, 16), 16)
                rt, rs = wide[0, part, :], wide[1, part, :]
                for j in range(span):
                    t, s = teach[part, lanes[j]], learn[part, lanes[j]]
                    v = jnp.exp(s - rs) - jnp.exp(t - rt) + jnp.exp(s - cs[j]) - jnp.exp(t - ct[j])
                    coupling[part, lanes[j]] = (0.5 * v).astype(BF)
                return inner

            lax.fori_loop(r * (chunk // 16), (r + 1) * (chunk // 16), step, 0)

        @pl.when(r == 0)
        def _():
            enter[9].wait()

        product[:chunk, :] = 100.0 * jnp.dot(
            coupling[part, :], cols[...].reshape(size, d), preferred_element_type=F32
        )
        for i in range(chunk // n):
            at = r * (chunk // n) + i
            dy = lax.rem(lax.div(at, NX) + NY - y, NY)
            dx = lax.rem(lax.rem(at, NX) + NX - x, NX)
            k = dy * (1 - c) + dx * c
            f = dx * (1 - c) + dy * c
            block = slice(i * n, (i + 1) * n)
            keep_image[f * 4 + k] = product[block, mine].astype(BF)
            give[k * 4 + f] = product[block, other].astype(BF)
        return carry

    lax.fori_loop(0, 4, chunk_step, 0)
    enter[8].wait()

    def text_step(i, carry):
        part = pl.ds(pl.multiple_of(i * chunk, chunk), chunk)
        product[part, :] = 100.0 * lax.dot_general(
            coupling[:, part],
            rows[...].reshape(size, d),
            (((0,), (0,)), ((), ())),
            preferred_element_type=F32,
        )
        return carry

    lax.fori_loop(0, 4, text_step, 0)
    out = 1 - 2 * c

    def text_block(k, core):
        at = lax.rem(z + NZ + k, NZ) * NC + core
        return product[pl.ds(pl.multiple_of(at * n, n), n), :]

    def put(i, v):
        v = v.astype(BF)
        give[16 + i] = v[:, :half]
        give[24 + i] = v[:, half:]

    put(0, text_block(0, 1 - c))
    put(1, text_block(4, 1 - c))
    keep_text[0] = text_block(0, c)
    keep_text[1] = text_block(4, c)
    for k in (1, 2, 3):
        for core in range(2):
            put(2 * k + core, text_block(-out * k, core))
            keep_text[2 * k + core] = text_block(out * k, core)


def pass_2(args, n, d):
    size = NY * NX * n
    vmem = pl.BlockSpec(memory_space=pltpu.VMEM)
    return pl.pallas_call(
        pass_2_kernel,
        out_shape=(
            jax.ShapeDtypeStruct((33, n, d // 2), BF),
            jax.ShapeDtypeStruct((16, n, d // 2), BF),
            jax.ShapeDtypeStruct((8, n, d), F32),
            jax.ShapeDtypeStruct((2, 8, LANES), F32),
        ),
        in_specs=[pl.BlockSpec(memory_space=pltpu.HBM)] * 2 + [vmem] * (len(args) - 2),
        out_specs=(vmem,) * 4,
        scratch_shapes=[
            pltpu.VMEM((size, size), F32),
            pltpu.VMEM((size, size), F32),
            pltpu.VMEM((16, n, d), BF),
            pltpu.VMEM((16, n, d), BF),
            pltpu.VMEM((size, size), BF),
            pltpu.VMEM((2, size, LANES), F32),
            pltpu.VMEM((size, d), F32),
            pltpu.SemaphoreType.DMA((10,)),
        ],
        compiler_params=pltpu.CompilerParams(vmem_limit_bytes=PASS_2_BYTES),
        cost_estimate=pl.CostEstimate(
            flops=4 * size * size * d, bytes_accessed=20 << 20, transcendentals=4 * size * size
        ),
    )(*args)


def vmem_call(kernel, outs, args):
    vmem = pl.BlockSpec(memory_space=pltpu.VMEM)
    return pl.pallas_call(
        kernel,
        out_shape=tuple(jax.ShapeDtypeStruct(s, t) for s, t in outs),
        in_specs=[vmem] * len(args),
        out_specs=(vmem,) * len(outs),
        compiler_params=pltpu.CompilerParams(vmem_limit_bytes=VMEM_BYTES),
        cost_estimate=pl.CostEstimate(flops=1 << 20, bytes_accessed=4 << 20, transcendentals=0),
    )(*args)


def pack(ref, row, lane, v):
    v = jnp.broadcast_to(v, (16, LANES))
    for k in range(3):
        piece = v.astype(BF)
        ref[row : row + 16, lane + k * LANES : lane + (k + 1) * LANES] = piece
        v = v - piece.astype(F32)


def unpack(ref, row, lane):
    v = ref[row : row + 16, lane : lane + 3 * LANES].astype(F32)
    return (v[:1, :LANES] + v[:1, LANES : 2 * LANES]) + v[:1, 2 * LANES :]


def choose(flag, a, b):
    return jnp.where(flag + jnp.zeros(a.shape, jnp.int32) == 0, a, b)


def load_kernel(
    keep_text, keep_image, got, loss_part,
    text_own, k1, k2, k34, image_own, p1, m1, far, rows_loss,
):
    z, _, _, _ = position()
    n, h = got.shape[1:]
    for i in range(8):
        for q in range(2):
            lanes = slice(q * h, (q + 1) * h)
            v = keep_text[i, :, lanes] + got[16 + 8 * q + i].astype(F32)
            if i == 0:
                text_own[:, lanes] = v
            elif i == 1:
                k34[2 * n : 3 * n, lanes] = v.astype(BF)
            elif i >= 6:
                k34[(i - 6) * n : (i - 5) * n, lanes] = v.astype(BF)
            else:
                (k1, k2)[i // 2 - 1][i % 2, :, lanes] = v
    image_own[0] = keep_image[0:4]
    image_own[1] = got[0:4]
    cols_loss = loss_part[1, :1]
    for f, out in ((1, p1), (2, far), (3, m1)):
        out[: 4 * n] = keep_image[f * 4 : f * 4 + 4].reshape(4 * n, h)
        out[4 * n : 8 * n] = got[f * 4 : f * 4 + 4].reshape(4 * n, h)
        out[8 * n :] = jnp.zeros((16, h), BF)
        pack(out, 8 * n, 0, cols_loss)
    sib = got[32].astype(F32)
    chip = loss_part[0, :1] + ((sib[0:1, :LANES] + sib[16:17, :LANES]) + sib[32:33, :LANES])
    lane = lax.broadcasted_iota(jnp.int32, (1, LANES), 1)
    mine = jnp.where(lane == z, chip, 0.0)
    rows_loss[...] = jnp.broadcast_to(mine, (8, LANES))
    k34[3 * n :] = jnp.zeros((16, 2 * h), BF)
    pack(k34, 3 * n, 0, mine)


def pass_on_kernel(k1, k2, k34, rows_loss, b1, b2):
    _, c, _, _ = position()
    n, d = k1.shape[1:]
    for core in range(2):
        part = slice(core * n, (core + 1) * n)
        b1[part] = (k1[core] + k34[part].astype(F32)).astype(BF)
        v = k34[2 * n : 3 * n].astype(F32)
        b2[part] = (k2[core] + choose(c - core, v, jnp.zeros_like(v))).astype(BF)
    came = unpack(k34, 3 * n, 0)
    for ref in (b1, b2):
        ref[2 * n :] = jnp.zeros((16, d), BF)
    pack(b1, 2 * n, 0, rows_loss[:1] + came)
    pack(b2, 2 * n, 0, came)


def ring_sum(odd, own, back, ahead, far):
    return (own + choose(odd, ahead, back)) + (far + choose(odd, back, ahead))


def line_kernel(own, p1, m1, far, loss_part, out, w1, w2, w3, cols_loss):
    _, c, y, x = position()
    n, h = own.shape[2:]
    for k, ref in enumerate((out, w1, w2, w3)):
        for core in range(2):
            part = slice((core * 4 + k) * n, (core * 4 + k + 1) * n)
            v = own[core, k].astype(F32) + far[part].astype(F32)
            v = v + p1[part].astype(F32) + m1[part].astype(F32)
            ref[core * n : (core + 1) * n] = v.astype(ref.dtype)
    odd = lax.rem(x * (1 - c) + y * c, 2)
    v = ring_sum(odd, loss_part[1, :1], *[unpack(r, 8 * n, 0) for r in (p1, m1, far)])
    cols_loss[...] = jnp.broadcast_to(v, (8, LANES))
    for ref in (w1, w2, w3):
        ref[2 * n :] = jnp.zeros((16, h), BF)
        pack(ref, 2 * n, 0, v)


def last_kernel(
    text_own, b1, b2, k34, rows_loss, line, w1, w2, w3, cols_loss,
    text, image, share, loss,
):
    _, c, y, x = position()
    n, d = text.shape
    ways = []
    for core in range(2):
        part = slice(core * n, (core + 1) * n)
        ways.append(b1[part].astype(F32) + b2[part].astype(F32))
    text[...] = text_own[...] + choose(c, ways[0], ways[1])
    share[:n, :d] = choose(c, ways[1], ways[0]).astype(BF)
    v = line[...]
    for r in (w1, w2, w3):
        v = v + r[: 2 * n].astype(F32)
    image[...] = v[:n].astype(BF)
    share[:n, d:] = v[n:].astype(BF)
    odd = lax.rem(y * (1 - c) + x * c, 2)
    cols = ring_sum(odd, cols_loss[:1], *[unpack(r, 2 * n, 0) for r in (w1, w3, w2)])
    near = unpack(k34, 3 * n, 0) + unpack(b1, 2 * n, 0)
    rows = choose(c, near + (rows_loss[:1] + unpack(b2, 2 * n, 0)), near)
    share[n:] = jnp.zeros((16, share.shape[1]), BF)
    pack(share, n, 0, rows)
    pack(share, n, 3 * LANES, cols)
    loss[0] = jnp.broadcast_to(rows, (8, LANES))
    loss[1] = jnp.broadcast_to(cols, (8, LANES))


def end_kernel(scale, text, image, share, loss, text_grad, image_grad, total):
    _, c, _, _ = position()
    n, d = text.shape
    h = d // 2
    text_grad[...] = (text[...] + share[:n, :d].astype(F32)).astype(BF)
    mine, other = image[...].astype(F32), share[:n, d:].astype(F32)
    image_grad[:, :h] = choose(c, mine, other).astype(BF)
    image_grad[:, h:] = choose(c, other, mine).astype(BF)
    rows = loss[0, :1] + unpack(share, n, 0)
    cols = choose(c, loss[1, :1], unpack(share, n, 3 * LANES))
    total[0] = (jnp.sum(rows) + jnp.max(cols)) * scale


def reduce_all(give, keep_image, keep_text, loss_part):
    n, d = keep_text.shape[1:]
    h = d // 2
    got = swap(give, c_bits=1)
    small = ((8, LANES), F32)
    pair, line_out = ((2, n, d), F32), ((8 * n + 16, h), BF)
    text_own, k1, k2, k34, image_own, p1, m1, far, rows_loss = vmem_call(
        load_kernel,
        [((n, d), F32), pair, pair, ((3 * n + 16, d), BF), ((2, 4, n, h), BF)]
        + [line_out] * 3
        + [small],
        (keep_text, keep_image, got, loss_part),
    )
    far = move_first(far, 2)
    k34 = move_z(k34, 2)
    p1 = move_first(p1, 1)
    m1 = move_first(m1, -1)
    b1, b2 = vmem_call(
        pass_on_kernel, [((2 * n + 16, d), BF)] * 2, (k1, k2, k34, rows_loss)
    )
    b1 = move_z(b1, 1)
    b2 = move_z(b2, 2)
    line, w1, w2, w3, cols_loss = vmem_call(
        line_kernel,
        [((2 * n, h), F32)] + [((2 * n + 16, h), BF)] * 3 + [small],
        (image_own, p1, m1, far, loss_part),
    )
    w1 = move_second(w1, 1)
    w2 = move_second(w2, 2)
    w3 = move_second(w3, -1)
    text, image, share, loss = vmem_call(
        last_kernel,
        [((n, d), F32), ((n, h), BF), ((n + 16, d + h), BF), ((2, 8, LANES), F32)],
        (text_own, b1, b2, k34, rows_loss, line, w1, w2, w3, cols_loss),
    )
    vmem = pl.BlockSpec(memory_space=pltpu.VMEM)
    scale = 0.5 / (n * NX * NY * NZ * NC)
    return pl.pallas_call(
        functools.partial(end_kernel, scale),
        out_shape=(
            jax.ShapeDtypeStruct((n, d), BF),
            jax.ShapeDtypeStruct((n, d), BF),
            jax.ShapeDtypeStruct((1,), F32),
        ),
        in_specs=[vmem] * 4,
        out_specs=(vmem, vmem, pl.BlockSpec(memory_space=pltpu.SMEM)),
        compiler_params=pltpu.CompilerParams(vmem_limit_bytes=VMEM_BYTES),
    )(text, image, swap(share, c_bits=1), loss)


def merge_steps(row_st, col_st):
    row_st = merged([row_st] + [swap(row_st, x_bits=b) for b in (1, 2, 3)])
    col_st = merged([col_st] + [swap(col_st, z_bits=b) for b in (1, 2, 3)])
    row_parts = [row_st] + [swap(row_st, y_bits=b) for b in (1, 2, 3)]
    col_st = merged([col_st, swap(col_st, z_bits=4)])
    return row_parts + [col_st, swap(col_st, c_bits=1)]


def per_device(teacher_image, teacher_text, student_image, student_text):
    n, d = teacher_image.shape
    core = lax.rem(lax.axis_index("row"), NC)
    keep = jnp.where(core == 0, teacher_image, student_image)
    give = jnp.where(core == 0, student_image, teacher_image)
    got = swap(jnp.stack([give, teacher_text, student_text]), c_bits=1)
    text_blocks = gather_cols(jnp.stack([jnp.stack([teacher_text, student_text]), got[1:]]))
    image_blocks = gather_rows(jnp.stack([keep, got[0]]))
    both, student, row_st, col_st = pass_1(
        list(image_blocks) + list(text_blocks), n, d
    )
    give, keep_image, keep_text, loss_part = pass_2(
        [both, student] + merge_steps(row_st, col_st), n, d
    )
    text_grad, image_grad, loss = reduce_all(give, keep_image, keep_text, loss_part)
    return (image_grad, text_grad, loss.reshape(()))


def solution(mesh):
    placed = P(("row", "col"), None)
    return jax.shard_map(
        per_device,
        mesh=mesh,
        in_specs=(placed,) * 4,
        out_specs=(placed, placed, P()),
        check_vma=False,
    )
```

```python
import functools

import jax
import jax.numpy as jnp
from jax import lax
from jax.experimental import pallas as pl
from jax.experimental.pallas import tpu as pltpu
from jax.sharding import PartitionSpec as P

NX, NY, NZ, NC = 4, 4, 8, 2
BF = jnp.bfloat16
F32 = jnp.float32
GROUP = 8
LANES = 128
VMEM_BYTES = 16 << 20
PASS_1_BYTES = 40 << 20
PASS_2_BYTES = 48 << 20


def place(z, c, y, x):
    return ((z % NZ * NC + c) * NY + y % NY) * NX + x % NX


def send(v, target):
    pairs = [
        (place(z, c, y, x), place(*target(z, c, y, x)))
        for z in range(NZ)
        for c in range(NC)
        for y in range(NY)
        for x in range(NX)
    ]
    return lax.ppermute(v, ("row", "col"), pairs)


def swap(v, z_bits=0, c_bits=0, y_bits=0, x_bits=0):
    return send(v, lambda z, c, y, x: (z ^ z_bits, c ^ c_bits, y ^ y_bits, x ^ x_bits))


def move_first(v, d):
    return send(v, lambda z, c, y, x: (z, c, y + d * c, x + d * (1 - c)))


def move_second(v, d):
    return send(v, lambda z, c, y, x: (z, c, y + d * (1 - c), x + d * c))


def move_z(v, d):
    return send(v, lambda z, c, y, x: (z + d * (1 - 2 * c), c, y, x))


def position():
    row, col = lax.axis_index("row"), lax.axis_index("col")
    return lax.div(row, NC), lax.rem(row, NC), lax.div(col, NX), lax.rem(col, NX)


def gather_rows(v):
    from_m = move_first(v, 1)
    from_p = move_first(v, -1)
    from_2 = move_first(v, 2)
    line = jnp.stack([v, from_p, from_2, from_m], axis=1)
    up = move_second(line, 1)
    down = move_second(line, -1)
    far_a = move_second(up[:, :2], 1)
    far_b = move_second(down[:, 2:], -1)
    got_1 = swap(jnp.stack([line[1], down[1], up[1]]), c_bits=1)
    got_2 = swap(jnp.concatenate([far_a[1], far_b[1]]), c_bits=1)
    return line, up, down, far_a, far_b, got_1, got_2


def gather_cols(v):
    out = [v]
    for _ in range(3):
        out.append(move_z(out[-1], 1))
    far = move_z(out[3][0], 1)
    back = swap(jnp.stack(out[1:3]), c_bits=1)
    return out + [far, back, swap(out[3], c_bits=1), swap(far, c_bits=1)]


def pass_1_kernel(
    line, up, down, far_a, far_b, got_1, got_2,
    t0, t1, t2, t3, far, back, b3, far_sib,
    both_out, student, row_st, col_st,
    teach, learn, rows, cols, tops, wide, sums, sem,
):
    z, c, y, x = position()
    n, d = rows.shape[2:]
    size = teach.shape[0]
    tiles = size // LANES

    def row_place(second, first):
        dy = second * (1 - c) + first * c
        dx = first * (1 - c) + second * c
        return lax.rem(y + dy, NY) * NX + lax.rem(x + dx, NX)

    def col_place(steps, core):
        return lax.rem(z + NZ + steps, NZ) * NC + core

    pieces = []
    for k in range(4):
        for f in range(4):
            if k == 2:
                src = (far_a, (0, f)) if f < 2 else (far_b, (0, f - 2))
            else:
                src = ({0: line, 1: down, 3: up}[k], (0, f))
            pieces.append((src, (rows, c, row_place(k, f))))
            src = {0: (got_1, (0, k)), 1: (got_1, (1, k)), 2: (got_2, k), 3: (got_1, (2, k))}[f]
            pieces.append((src, (rows, 1 - c, row_place(k, f))))
    way = 2 * c - 1
    for kind in range(2):
        for j, ref in enumerate((t0, t1, t2, t3)):
            for dc in range(2):
                core = c if dc == 0 else 1 - c
                pieces.append(((ref, (dc, kind)), (cols, kind, col_place(way * j, core))))
        for j in range(3):
            for dc in range(2):
                core = 1 - c if dc == 0 else c
                src = (back, (j, dc, kind)) if j < 2 else (b3, (dc, kind))
                pieces.append((src, (cols, kind, col_place(-way * (j + 1), core))))
        pieces.append(((far, kind), (cols, kind, col_place(4, c))))
        pieces.append(((far_sib, kind), (cols, kind, col_place(4, 1 - c))))
    for (src, i), (dst, j, k) in pieces:
        dst[j, k] = src[i]
    leave = [
        pltpu.make_async_copy(rows.at[1], student.at[0], sem.at[0]),
        pltpu.make_async_copy(cols.at[1], student.at[1], sem.at[1]),
    ]
    for copy in leave:
        copy.start()

    for kind, buf in ((0, teach), (1, learn)):
        buf[...] = 100.0 * lax.dot_general(
            rows[kind].reshape(size, d),
            cols[kind].reshape(size, d),
            (((1,), (1,)), ((), ())),
            preferred_element_type=F32,
        )
        copy = pltpu.make_async_copy(buf, both_out.at[kind], sem.at[2 + kind])
        copy.start()
        leave.append(copy)

    def tile(ref, part, q):
        return ref[part, q * LANES : (q + 1) * LANES]

    def top_step(i, carry):
        part = pl.ds(pl.multiple_of(i * GROUP, GROUP), GROUP)
        out = []
        for k, ref in ((0, teach), (1, learn)):
            v = [tile(ref, part, q) for q in range(tiles)]
            out.append([jnp.maximum(a, b) for a, b in zip(carry[k], v)])
            while len(v) > 1:
                v = [jnp.maximum(a, b) for a, b in zip(v[::2], v[1::2])]
            tops[k, part, :] = v[0]
        return out

    low = jnp.full((GROUP, LANES), -jnp.inf, F32)
    col_tops = lax.fori_loop(0, size // GROUP, top_step, [[low] * tiles] * 2, unroll=4)
    col_tops = [[jnp.max(v, axis=0, keepdims=True) for v in tops_k] for tops_k in col_tops]
    row_tops = []
    for k in range(2):
        top = jnp.max(tops[k].T, axis=0, keepdims=True)
        row_tops.append(top)
        wide[k] = jnp.broadcast_to(top, (LANES, size)).T

    for h in range(2):
        span = range(h * tiles // 2, (h + 1) * tiles // 2)
        t_tops = [jnp.broadcast_to(col_tops[0][q], (GROUP, LANES)) for q in span]
        s_tops = [jnp.broadcast_to(col_tops[1][q], (GROUP, LANES)) for q in span]

        def sum_step(i, carry):
            part = pl.ds(pl.multiple_of(i * GROUP, GROUP), GROUP)
            rt, rs = wide[0, part, :], wide[1, part, :]
            acc = [0.0, 0.0, 0.0] if h == 0 else [sums[k, part, :] for k in range(3)]
            out = []
            for j, q in enumerate(span):
                t, s = tile(teach, part, q), tile(learn, part, q)
                gap = t - s
                e = jnp.exp(t - rt)
                acc = [acc[0] + e, acc[1] + jnp.exp(s - rs), acc[2] + e * gap]
                e = jnp.exp(t - t_tops[j])
                a, b, w = carry[j]
                out.append((a + e, b + jnp.exp(s - s_tops[j]), w + e * gap))
            for k in range(3):
                sums[k, part, :] = acc[k]
            return out

        none = jnp.zeros((GROUP, LANES), F32)
        out = lax.fori_loop(0, size // GROUP, sum_step, [(none,) * 3] * len(span), unroll=8)
        for j, q in enumerate(span):
            a, b, w = [jnp.sum(v, axis=0, keepdims=True) for v in out[j]]
            zero = jnp.zeros_like(w)
            col_st[:, q * LANES : (q + 1) * LANES] = jnp.concatenate(
                [col_tops[0][q], a, col_tops[1][q], b, w, zero, zero, zero], axis=0
            )
    a, b, w = [jnp.sum(sums[k].T, axis=0, keepdims=True) for k in range(3)]
    zero = jnp.zeros_like(w)
    row_st[...] = jnp.concatenate([row_tops[0], a, row_tops[1], b, w, zero, zero, zero], axis=0)
    for copy in leave:
        copy.wait()


def pass_1(pieces, n, d):
    size = NY * NX * n
    vmem = pl.BlockSpec(memory_space=pltpu.VMEM)
    hbm = pl.BlockSpec(memory_space=pltpu.HBM)
    both = jax.ShapeDtypeStruct((2, size, size), F32)
    blocks = jax.ShapeDtypeStruct((2, 16, n, d), BF)
    small = jax.ShapeDtypeStruct((8, size), F32)
    return pl.pallas_call(
        pass_1_kernel,
        out_shape=(both, blocks, small, small),
        in_specs=[vmem] * len(pieces),
        out_specs=(hbm, hbm, vmem, vmem),
        scratch_shapes=[
            pltpu.VMEM((size, size), F32),
            pltpu.VMEM((size, size), F32),
            pltpu.VMEM((2, 16, n, d), BF),
            pltpu.VMEM((2, 16, n, d), BF),
            pltpu.VMEM((2, size, LANES), F32),
            pltpu.VMEM((2, size, LANES), F32),
            pltpu.VMEM((3, size, LANES), F32),
            pltpu.SemaphoreType.DMA((4,)),
        ],
        compiler_params=pltpu.CompilerParams(vmem_limit_bytes=PASS_1_BYTES),
        cost_estimate=pl.CostEstimate(
            flops=4 * size * size * d, bytes_accessed=20 << 20, transcendentals=4 * size * size
        ),
    )(*pieces)


def merge(parts):
    parts = [[p[k : k + 1] for k in range(5)] for p in parts]
    t_top = parts[0][0]
    s_top = parts[0][2]
    for p in parts[1:]:
        t_top = jnp.maximum(t_top, p[0])
        s_top = jnp.maximum(s_top, p[2])
    terms = []
    for p in parts:
        a = jnp.exp(p[0] - t_top)
        terms.append((p[1] * a, p[3] * jnp.exp(p[2] - s_top), p[4] * a))
    while len(terms) > 1:
        terms = [
            tuple(u + v for u, v in zip(terms[i], terms[i + 1])) for i in range(0, len(terms), 2)
        ]
    t_sum, s_sum, w = terms[0]
    return [t_top, t_sum, s_top, s_sum, w]


def merged(parts):
    return jnp.concatenate(merge(parts), axis=0)


def pass_2_kernel(
    both_in, student_in, ra, rb, rc, rd, ca, cb,
    give, keep_image, keep_text, loss_part,
    teach, learn, rows, cols, coupling, wide, product, sem,
):
    z, c, y, x = position()
    n, d = rows.shape[1:]
    size = teach.shape[0]
    half = d // 2
    chunk = size // 4
    enter = []
    for r in range(4):
        part = pl.ds(r * chunk, chunk)
        for k, dst in ((0, teach), (1, learn)):
            enter.append(pltpu.make_async_copy(both_in.at[k, part], dst.at[part], sem.at[len(enter)]))
    enter.append(pltpu.make_async_copy(student_in.at[0], rows, sem.at[8]))
    enter.append(pltpu.make_async_copy(student_in.at[1], cols, sem.at[9]))
    for i in (0, 1, 9, 2, 3, 4, 5, 6, 7, 8):
        enter[i].start()
    row_st = merge([r[...] for r in (ra, rb, rc, rd)])
    col_st = merge([r[...] for r in (ca, cb)])
    row_t, row_s = row_st[0] + jnp.log(row_st[1]), row_st[2] + jnp.log(row_st[3])
    col_t, col_s = col_st[0] + jnp.log(col_st[1]), col_st[2] + jnp.log(col_st[3])
    part_r = jnp.sum(row_st[4] / row_st[1] + (row_s - row_t), axis=1, keepdims=True)
    part_c = jnp.sum(col_st[4] / col_st[1] + (col_s - col_t), axis=1, keepdims=True)
    loss_part[0] = jnp.broadcast_to(part_r, (8, LANES))
    loss_part[1] = jnp.broadcast_to(part_c, (8, LANES))
    whole = jnp.broadcast_to(part_r, (16, half))
    for k in range(3):
        piece = whole.astype(BF)
        give[32, 16 * k : 16 * k + 16] = piece
        whole = whole - piece.astype(F32)
    give[32, 48:] = jnp.zeros((n - 48, half), BF)
    for k, v in ((0, row_t), (1, row_s)):
        wide[k] = jnp.broadcast_to(v, (LANES, size)).T

    span = 4
    mine = pl.ds(pl.multiple_of(c * half, half), half)
    other = pl.ds(pl.multiple_of((1 - c) * half, half), half)

    def chunk_step(r, carry):
        part = pl.ds(pl.multiple_of(r * chunk, chunk), chunk)
        pltpu.make_async_copy(both_in.at[0, part], teach.at[part], sem.at[2 * r]).wait()
        pltpu.make_async_copy(both_in.at[1, part], learn.at[part], sem.at[2 * r + 1]).wait()
        for h in range(size // (span * LANES)):
            lanes = [slice((h * span + j) * LANES, (h * span + j + 1) * LANES) for j in range(span)]
            ct = [jnp.broadcast_to(col_t[:, s], (16, LANES)) for s in lanes]
            cs = [jnp.broadcast_to(col_s[:, s], (16, LANES)) for s in lanes]

            def step(i, inner):
                part = pl.ds(pl.multiple_of(r * chunk + i * 16, 16), 16)
                rt, rs = wide[0, part, :], wide[1, part, :]
                for j in range(span):
                    t, s = teach[part, lanes[j]], learn[part, lanes[j]]
                    v = jnp.exp(s - rs) - jnp.exp(t - rt) + jnp.exp(s - cs[j]) - jnp.exp(t - ct[j])
                    coupling[part, lanes[j]] = (0.5 * v).astype(BF)
                return inner

            lax.fori_loop(0, chunk // 16, step, 0, unroll=8)

        @pl.when(r == 0)
        def _():
            enter[9].wait()

        product[:chunk, :] = 100.0 * jnp.dot(
            coupling[part, :], cols[...].reshape(size, d), preferred_element_type=F32
        )
        for i in range(chunk // n):
            at = r * (chunk // n) + i
            dy = lax.rem(lax.div(at, NX) + NY - y, NY)
            dx = lax.rem(lax.rem(at, NX) + NX - x, NX)
            k = dy * (1 - c) + dx * c
            f = dx * (1 - c) + dy * c
            block = slice(i * n, (i + 1) * n)
            keep_image[f * 4 + k] = product[block, mine].astype(BF)
            give[k * 4 + f] = product[block, other].astype(BF)
        return carry

    lax.fori_loop(0, 4, chunk_step, 0)
    enter[8].wait()

    def text_step(i, carry):
        part = pl.ds(pl.multiple_of(i * 2 * chunk, 2 * chunk), 2 * chunk)
        product[part, :] = 100.0 * lax.dot_general(
            coupling[:, part],
            rows[...].reshape(size, d),
            (((0,), (0,)), ((), ())),
            preferred_element_type=F32,
        )
        return carry

    lax.fori_loop(0, 2, text_step, 0)
    out = 1 - 2 * c

    def text_block(k, core):
        at = lax.rem(z + NZ + k, NZ) * NC + core
        return product[pl.ds(pl.multiple_of(at * n, n), n), :]

    def put(i, v):
        v = v.astype(BF)
        give[16 + i] = v[:, :half]
        give[24 + i] = v[:, half:]

    put(0, text_block(0, 1 - c))
    put(1, text_block(4, 1 - c))
    keep_text[0] = text_block(0, c)
    keep_text[1] = text_block(4, c)
    for k in (1, 2, 3):
        for core in range(2):
            put(2 * k + core, text_block(-out * k, core))
            keep_text[2 * k + core] = text_block(out * k, core)


def pass_2(args, n, d):
    size = NY * NX * n
    vmem = pl.BlockSpec(memory_space=pltpu.VMEM)
    return pl.pallas_call(
        pass_2_kernel,
        out_shape=(
            jax.ShapeDtypeStruct((33, n, d // 2), BF),
            jax.ShapeDtypeStruct((16, n, d // 2), BF),
            jax.ShapeDtypeStruct((8, n, d), F32),
            jax.ShapeDtypeStruct((2, 8, LANES), F32),
        ),
        in_specs=[pl.BlockSpec(memory_space=pltpu.HBM)] * 2 + [vmem] * (len(args) - 2),
        out_specs=(vmem,) * 4,
        scratch_shapes=[
            pltpu.VMEM((size, size), F32),
            pltpu.VMEM((size, size), F32),
            pltpu.VMEM((16, n, d), BF),
            pltpu.VMEM((16, n, d), BF),
            pltpu.VMEM((size, size), BF),
            pltpu.VMEM((2, size, LANES), F32),
            pltpu.VMEM((size, d), F32),
            pltpu.SemaphoreType.DMA((10,)),
        ],
        compiler_params=pltpu.CompilerParams(vmem_limit_bytes=PASS_2_BYTES),
        cost_estimate=pl.CostEstimate(
            flops=4 * size * size * d, bytes_accessed=20 << 20, transcendentals=4 * size * size
        ),
    )(*args)


def vmem_call(kernel, outs, args):
    vmem = pl.BlockSpec(memory_space=pltpu.VMEM)
    return pl.pallas_call(
        kernel,
        out_shape=tuple(jax.ShapeDtypeStruct(s, t) for s, t in outs),
        in_specs=[vmem] * len(args),
        out_specs=(vmem,) * len(outs),
        compiler_params=pltpu.CompilerParams(vmem_limit_bytes=VMEM_BYTES),
        cost_estimate=pl.CostEstimate(flops=1 << 20, bytes_accessed=4 << 20, transcendentals=0),
    )(*args)


def pack(ref, row, lane, v):
    v = jnp.broadcast_to(v, (16, LANES))
    for k in range(3):
        piece = v.astype(BF)
        ref[row : row + 16, lane + k * LANES : lane + (k + 1) * LANES] = piece
        v = v - piece.astype(F32)


def unpack(ref, row, lane):
    v = ref[row : row + 16, lane : lane + 3 * LANES].astype(F32)
    return (v[:1, :LANES] + v[:1, LANES : 2 * LANES]) + v[:1, 2 * LANES :]


def choose(flag, a, b):
    return jnp.where(flag + jnp.zeros(a.shape, jnp.int32) == 0, a, b)


def load_kernel(
    keep_text, keep_image, got, loss_part,
    text_own, k1, k2, k34, image_own, p1, m1, far, rows_loss,
):
    z, _, _, _ = position()
    n, h = got.shape[1:]
    for i in range(8):
        for q in range(2):
            lanes = slice(q * h, (q + 1) * h)
            v = keep_text[i, :, lanes] + got[16 + 8 * q + i].astype(F32)
            if i == 0:
                text_own[:, lanes] = v
            elif i == 1:
                k34[2 * n : 3 * n, lanes] = v.astype(BF)
            elif i >= 6:
                k34[(i - 6) * n : (i - 5) * n, lanes] = v.astype(BF)
            else:
                (k1, k2)[i // 2 - 1][i % 2, :, lanes] = v
    image_own[0] = keep_image[0:4]
    image_own[1] = got[0:4]
    cols_loss = loss_part[1, :1]
    for f, out in ((1, p1), (2, far), (3, m1)):
        out[: 4 * n] = keep_image[f * 4 : f * 4 + 4].reshape(4 * n, h)
        out[4 * n : 8 * n] = got[f * 4 : f * 4 + 4].reshape(4 * n, h)
        out[8 * n :] = jnp.zeros((16, h), BF)
        pack(out, 8 * n, 0, cols_loss)
    sib = got[32].astype(F32)
    chip = loss_part[0, :1] + ((sib[0:1, :LANES] + sib[16:17, :LANES]) + sib[32:33, :LANES])
    lane = lax.broadcasted_iota(jnp.int32, (1, LANES), 1)
    mine = jnp.where(lane == z, chip, 0.0)
    rows_loss[...] = jnp.broadcast_to(mine, (8, LANES))
    k34[3 * n :] = jnp.zeros((16, 2 * h), BF)
    pack(k34, 3 * n, 0, mine)


def pass_on_kernel(k1, k2, k34, rows_loss, b1, b2):
    _, c, _, _ = position()
    n, d = k1.shape[1:]
    for core in range(2):
        part = slice(core * n, (core + 1) * n)
        b1[part] = (k1[core] + k34[part].astype(F32)).astype(BF)
        v = k34[2 * n : 3 * n].astype(F32)
        b2[part] = (k2[core] + choose(c - core, v, jnp.zeros_like(v))).astype(BF)
    came = unpack(k34, 3 * n, 0)
    for ref in (b1, b2):
        ref[2 * n :] = jnp.zeros((16, d), BF)
    pack(b1, 2 * n, 0, rows_loss[:1] + came)
    pack(b2, 2 * n, 0, came)


def ring_sum(odd, own, back, ahead, far):
    return (own + choose(odd, ahead, back)) + (far + choose(odd, back, ahead))


def line_kernel(own, p1, m1, far, loss_part, out, w1, w2, w3, cols_loss):
    _, c, y, x = position()
    n, h = own.shape[2:]
    for k, ref in enumerate((out, w1, w2, w3)):
        for core in range(2):
            part = slice((core * 4 + k) * n, (core * 4 + k + 1) * n)
            v = own[core, k].astype(F32) + far[part].astype(F32)
            v = v + p1[part].astype(F32) + m1[part].astype(F32)
            ref[core * n : (core + 1) * n] = v.astype(ref.dtype)
    odd = lax.rem(x * (1 - c) + y * c, 2)
    v = ring_sum(odd, loss_part[1, :1], *[unpack(r, 8 * n, 0) for r in (p1, m1, far)])
    cols_loss[...] = jnp.broadcast_to(v, (8, LANES))
    for ref in (w1, w2, w3):
        ref[2 * n :] = jnp.zeros((16, h), BF)
        pack(ref, 2 * n, 0, v)


def last_kernel(
    text_own, b1, b2, k34, rows_loss, line, w1, w2, w3, cols_loss,
    text, image, share, loss,
):
    _, c, y, x = position()
    n, d = text.shape
    ways = []
    for core in range(2):
        part = slice(core * n, (core + 1) * n)
        ways.append(b1[part].astype(F32) + b2[part].astype(F32))
    text[...] = text_own[...] + choose(c, ways[0], ways[1])
    share[:n, :d] = choose(c, ways[1], ways[0]).astype(BF)
    v = line[...]
    for r in (w1, w2, w3):
        v = v + r[: 2 * n].astype(F32)
    image[...] = v[:n].astype(BF)
    share[:n, d:] = v[n:].astype(BF)
    odd = lax.rem(y * (1 - c) + x * c, 2)
    cols = ring_sum(odd, cols_loss[:1], *[unpack(r, 2 * n, 0) for r in (w1, w3, w2)])
    near = unpack(k34, 3 * n, 0) + unpack(b1, 2 * n, 0)
    rows = choose(c, near + (rows_loss[:1] + unpack(b2, 2 * n, 0)), near)
    share[n:] = jnp.zeros((16, share.shape[1]), BF)
    pack(share, n, 0, rows)
    pack(share, n, 3 * LANES, cols)
    loss[0] = jnp.broadcast_to(rows, (8, LANES))
    loss[1] = jnp.broadcast_to(cols, (8, LANES))


def end_kernel(scale, text, image, share, loss, text_grad, image_grad, total):
    _, c, _, _ = position()
    n, d = text.shape
    h = d // 2
    text_grad[...] = (text[...] + share[:n, :d].astype(F32)).astype(BF)
    mine, other = image[...].astype(F32), share[:n, d:].astype(F32)
    image_grad[:, :h] = choose(c, mine, other).astype(BF)
    image_grad[:, h:] = choose(c, other, mine).astype(BF)
    rows = loss[0, :1] + unpack(share, n, 0)
    cols = choose(c, loss[1, :1], unpack(share, n, 3 * LANES))
    total[0] = (jnp.sum(rows) + jnp.max(cols)) * scale


def reduce_all(give, keep_image, keep_text, loss_part):
    n, d = keep_text.shape[1:]
    h = d // 2
    got = swap(give, c_bits=1)
    small = ((8, LANES), F32)
    pair, line_out = ((2, n, d), F32), ((8 * n + 16, h), BF)
    text_own, k1, k2, k34, image_own, p1, m1, far, rows_loss = vmem_call(
        load_kernel,
        [((n, d), F32), pair, pair, ((3 * n + 16, d), BF), ((2, 4, n, h), BF)]
        + [line_out] * 3
        + [small],
        (keep_text, keep_image, got, loss_part),
    )
    far = move_first(far, 2)
    k34 = move_z(k34, 2)
    p1 = move_first(p1, 1)
    m1 = move_first(m1, -1)
    b1, b2 = vmem_call(
        pass_on_kernel, [((2 * n + 16, d), BF)] * 2, (k1, k2, k34, rows_loss)
    )
    b1 = move_z(b1, 1)
    b2 = move_z(b2, 2)
    line, w1, w2, w3, cols_loss = vmem_call(
        line_kernel,
        [((2 * n, h), F32)] + [((2 * n + 16, h), BF)] * 3 + [small],
        (image_own, p1, m1, far, loss_part),
    )
    w1 = move_second(w1, 1)
    w2 = move_second(w2, 2)
    w3 = move_second(w3, -1)
    text, image, share, loss = vmem_call(
        last_kernel,
        [((n, d), F32), ((n, h), BF), ((n + 16, d + h), BF), ((2, 8, LANES), F32)],
        (text_own, b1, b2, k34, rows_loss, line, w1, w2, w3, cols_loss),
    )
    vmem = pl.BlockSpec(memory_space=pltpu.VMEM)
    scale = 0.5 / (n * NX * NY * NZ * NC)
    return pl.pallas_call(
        functools.partial(end_kernel, scale),
        out_shape=(
            jax.ShapeDtypeStruct((n, d), BF),
            jax.ShapeDtypeStruct((n, d), BF),
            jax.ShapeDtypeStruct((1,), F32),
        ),
        in_specs=[vmem] * 4,
        out_specs=(vmem, vmem, pl.BlockSpec(memory_space=pltpu.SMEM)),
        compiler_params=pltpu.CompilerParams(vmem_limit_bytes=VMEM_BYTES),
    )(text, image, swap(share, c_bits=1), loss)


def merge_steps(row_st, col_st):
    row_st = merged([row_st] + [swap(row_st, x_bits=b) for b in (1, 2, 3)])
    col_st = merged([col_st] + [swap(col_st, z_bits=b) for b in (1, 2, 3)])
    row_parts = [row_st] + [swap(row_st, y_bits=b) for b in (1, 2, 3)]
    col_st = merged([col_st, swap(col_st, z_bits=4)])
    return row_parts + [col_st, swap(col_st, c_bits=1)]


def per_device(teacher_image, teacher_text, student_image, student_text):
    n, d = teacher_image.shape
    core = lax.rem(lax.axis_index("row"), NC)
    keep = jnp.where(core == 0, teacher_image, student_image)
    give = jnp.where(core == 0, student_image, teacher_image)
    texts = [teacher_text, student_text]
    texts = texts + [swap(v, c_bits=1) for v in texts]
    text = jnp.stack(texts).reshape(2, 2, n, d)
    text_blocks = gather_cols(text)
    image_blocks = gather_rows(jnp.stack([keep, swap(give, c_bits=1)]))
    both, student, row_st, col_st = pass_1(
        list(image_blocks) + list(text_blocks), n, d
    )
    give, keep_image, keep_text, loss_part = pass_2(
        [both, student] + merge_steps(row_st, col_st), n, d
    )
    text_grad, image_grad, loss = reduce_all(give, keep_image, keep_text, loss_part)
    return (image_grad, text_grad, loss.reshape(()))


def solution(mesh):
    placed = P(("row", "col"), None)
    return jax.shard_map(
        per_device,
        mesh=mesh,
        in_specs=(placed,) * 4,
        out_specs=(placed, placed, P()),
        check_vma=False,
    )
```

```python
import functools

import jax
import jax.numpy as jnp
from jax import lax
from jax.experimental import pallas as pl
from jax.experimental.pallas import tpu as pltpu
from jax.sharding import PartitionSpec as P

NX, NY, NZ, NC = 4, 4, 8, 2
BF = jnp.bfloat16
F32 = jnp.float32
GROUP = 8
LANES = 128
VMEM_BYTES = 16 << 20
PASS_1_BYTES = 40 << 20
PASS_2_BYTES = 48 << 20


def place(z, c, y, x):
    return ((z % NZ * NC + c) * NY + y % NY) * NX + x % NX


def send(v, target):
    pairs = [
        (place(z, c, y, x), place(*target(z, c, y, x)))
        for z in range(NZ)
        for c in range(NC)
        for y in range(NY)
        for x in range(NX)
    ]
    return lax.ppermute(v, ("row", "col"), pairs)


def swap(v, z_bits=0, c_bits=0, y_bits=0, x_bits=0):
    return send(v, lambda z, c, y, x: (z ^ z_bits, c ^ c_bits, y ^ y_bits, x ^ x_bits))


def move_first(v, d):
    return send(v, lambda z, c, y, x: (z, c, y + d * c, x + d * (1 - c)))


def move_second(v, d):
    return send(v, lambda z, c, y, x: (z, c, y + d * (1 - c), x + d * c))


def move_z(v, d):
    return send(v, lambda z, c, y, x: (z + d * (1 - 2 * c), c, y, x))


def position():
    row, col = lax.axis_index("row"), lax.axis_index("col")
    return lax.div(row, NC), lax.rem(row, NC), lax.div(col, NX), lax.rem(col, NX)


def gather_rows(v):
    from_m = move_first(v, 1)
    from_p = move_first(v, -1)
    from_2 = move_first(v, 2)
    line = jnp.stack([v, from_p, from_2, from_m], axis=1)
    up = move_second(line, 1)
    down = move_second(line, -1)
    far_a = move_second(up[:, :2], 1)
    far_b = move_second(down[:, 2:], -1)
    got_1 = swap(jnp.stack([line[1], down[1], up[1]]), c_bits=1)
    got_2 = swap(jnp.concatenate([far_a[1], far_b[1]]), c_bits=1)
    return line, up, down, far_a, far_b, got_1, got_2


def gather_cols(v):
    out = [v]
    for _ in range(3):
        out.append(move_z(out[-1], 1))
    far = move_z(out[3][0], 1)
    back = swap(jnp.stack(out[1:3]), c_bits=1)
    return out + [far, back, swap(out[3], c_bits=1), swap(far, c_bits=1)]


def pass_1_kernel(
    line, up, down, far_a, far_b, got_1, got_2,
    t0, t1, t2, t3, far, back, b3, far_sib,
    both_out, student, row_st, col_st,
    teach, learn, rows, cols, tops, wide, sums, sem,
):
    z, c, y, x = position()
    n, d = rows.shape[2:]
    size = teach.shape[0]
    tiles = size // LANES

    def row_place(second, first):
        dy = second * (1 - c) + first * c
        dx = first * (1 - c) + second * c
        return lax.rem(y + dy, NY) * NX + lax.rem(x + dx, NX)

    def col_place(steps, core):
        return lax.rem(z + NZ + steps, NZ) * NC + core

    pieces = []
    for k in range(4):
        for f in range(4):
            if k == 2:
                src = (far_a, (0, f)) if f < 2 else (far_b, (0, f - 2))
            else:
                src = ({0: line, 1: down, 3: up}[k], (0, f))
            pieces.append((src, (rows, c, row_place(k, f))))
            src = {0: (got_1, (0, k)), 1: (got_1, (1, k)), 2: (got_2, k), 3: (got_1, (2, k))}[f]
            pieces.append((src, (rows, 1 - c, row_place(k, f))))
    way = 2 * c - 1
    for kind in range(2):
        for j, ref in enumerate((t0, t1, t2, t3)):
            for dc in range(2):
                core = c if dc == 0 else 1 - c
                pieces.append(((ref, (dc, kind)), (cols, kind, col_place(way * j, core))))
        for j in range(3):
            for dc in range(2):
                core = 1 - c if dc == 0 else c
                src = (back, (j, dc, kind)) if j < 2 else (b3, (dc, kind))
                pieces.append((src, (cols, kind, col_place(-way * (j + 1), core))))
        pieces.append(((far, kind), (cols, kind, col_place(4, c))))
        pieces.append(((far_sib, kind), (cols, kind, col_place(4, 1 - c))))
    for (src, i), (dst, j, k) in pieces:
        dst[j, k] = src[i]
    leave = [
        pltpu.make_async_copy(rows.at[1], student.at[0], sem.at[0]),
        pltpu.make_async_copy(cols.at[1], student.at[1], sem.at[1]),
    ]
    for copy in leave:
        copy.start()

    for kind, buf in ((0, teach), (1, learn)):
        buf[...] = 100.0 * lax.dot_general(
            rows[kind].reshape(size, d),
            cols[kind].reshape(size, d),
            (((1,), (1,)), ((), ())),
            preferred_element_type=F32,
        )
        copy = pltpu.make_async_copy(buf, both_out.at[kind], sem.at[2 + kind])
        copy.start()
        leave.append(copy)

    def tile(ref, part, q):
        return ref[part, q * LANES : (q + 1) * LANES]

    def top_step(i, carry):
        part = pl.ds(pl.multiple_of(i * GROUP, GROUP), GROUP)
        out = []
        for k, ref in ((0, teach), (1, learn)):
            v = [tile(ref, part, q) for q in range(tiles)]
            out.append([jnp.maximum(a, b) for a, b in zip(carry[k], v)])
            while len(v) > 1:
                v = [jnp.maximum(a, b) for a, b in zip(v[::2], v[1::2])]
            tops[k, part, :] = v[0]
        return out

    low = jnp.full((GROUP, LANES), -jnp.inf, F32)
    col_tops = lax.fori_loop(0, size // GROUP, top_step, [[low] * tiles] * 2, unroll=4)
    col_tops = [[jnp.max(v, axis=0, keepdims=True) for v in tops_k] for tops_k in col_tops]
    row_tops = []
    for k in range(2):
        top = jnp.max(tops[k].T, axis=0, keepdims=True)
        row_tops.append(top)
        wide[k] = jnp.broadcast_to(top, (LANES, size)).T

    for h in range(2):
        span = range(h * tiles // 2, (h + 1) * tiles // 2)
        t_tops = [jnp.broadcast_to(col_tops[0][q], (GROUP, LANES)) for q in span]
        s_tops = [jnp.broadcast_to(col_tops[1][q], (GROUP, LANES)) for q in span]

        def sum_step(i, carry):
            part = pl.ds(pl.multiple_of(i * GROUP, GROUP), GROUP)
            rt, rs = wide[0, part, :], wide[1, part, :]
            acc = [0.0, 0.0, 0.0] if h == 0 else [sums[k, part, :] for k in range(3)]
            out = []
            for j, q in enumerate(span):
                t, s = tile(teach, part, q), tile(learn, part, q)
                gap = t - s
                e = jnp.exp(t - rt)
                acc = [acc[0] + e, acc[1] + jnp.exp(s - rs), acc[2] + e * gap]
                e = jnp.exp(t - t_tops[j])
                a, b, w = carry[j]
                out.append((a + e, b + jnp.exp(s - s_tops[j]), w + e * gap))
            for k in range(3):
                sums[k, part, :] = acc[k]
            return out

        none = jnp.zeros((GROUP, LANES), F32)
        out = lax.fori_loop(0, size // GROUP, sum_step, [(none,) * 3] * len(span), unroll=8)
        for j, q in enumerate(span):
            a, b, w = [jnp.sum(v, axis=0, keepdims=True) for v in out[j]]
            zero = jnp.zeros_like(w)
            col_st[:, q * LANES : (q + 1) * LANES] = jnp.concatenate(
                [col_tops[0][q], a, col_tops[1][q], b, w, zero, zero, zero], axis=0
            )
    a, b, w = [jnp.sum(sums[k].T, axis=0, keepdims=True) for k in range(3)]
    zero = jnp.zeros_like(w)
    row_st[...] = jnp.concatenate([row_tops[0], a, row_tops[1], b, w, zero, zero, zero], axis=0)
    for copy in leave:
        copy.wait()


def pass_1(pieces, n, d):
    size = NY * NX * n
    vmem = pl.BlockSpec(memory_space=pltpu.VMEM)
    hbm = pl.BlockSpec(memory_space=pltpu.HBM)
    both = jax.ShapeDtypeStruct((2, size, size), F32)
    blocks = jax.ShapeDtypeStruct((2, 16, n, d), BF)
    small = jax.ShapeDtypeStruct((8, size), F32)
    return pl.pallas_call(
        pass_1_kernel,
        out_shape=(both, blocks, small, small),
        in_specs=[vmem] * len(pieces),
        out_specs=(hbm, hbm, vmem, vmem),
        scratch_shapes=[
            pltpu.VMEM((size, size), F32),
            pltpu.VMEM((size, size), F32),
            pltpu.VMEM((2, 16, n, d), BF),
            pltpu.VMEM((2, 16, n, d), BF),
            pltpu.VMEM((2, size, LANES), F32),
            pltpu.VMEM((2, size, LANES), F32),
            pltpu.VMEM((3, size, LANES), F32),
            pltpu.SemaphoreType.DMA((4,)),
        ],
        compiler_params=pltpu.CompilerParams(vmem_limit_bytes=PASS_1_BYTES),
        cost_estimate=pl.CostEstimate(
            flops=4 * size * size * d, bytes_accessed=20 << 20, transcendentals=4 * size * size
        ),
    )(*pieces)


def merge(parts):
    parts = [[p[k : k + 1] for k in range(5)] for p in parts]
    t_top = parts[0][0]
    s_top = parts[0][2]
    for p in parts[1:]:
        t_top = jnp.maximum(t_top, p[0])
        s_top = jnp.maximum(s_top, p[2])
    terms = []
    for p in parts:
        a = jnp.exp(p[0] - t_top)
        terms.append((p[1] * a, p[3] * jnp.exp(p[2] - s_top), p[4] * a))
    while len(terms) > 1:
        terms = [
            tuple(u + v for u, v in zip(terms[i], terms[i + 1])) for i in range(0, len(terms), 2)
        ]
    t_sum, s_sum, w = terms[0]
    return [t_top, t_sum, s_top, s_sum, w]


def merged(parts):
    return jnp.concatenate(merge(parts), axis=0)


def pass_2_kernel(
    both_in, student_in, ra, rb, rc, rd, ca, cb,
    give, give_text, keep_image, keep_text, loss_part,
    teach, learn, rows, cols, coupling, wide, product, sem,
):
    z, c, y, x = position()
    n, d = rows.shape[1:]
    size = teach.shape[0]
    half = d // 2
    chunk = size // 4
    enter = []
    for r in range(4):
        part = pl.ds(r * chunk, chunk)
        for k, dst in ((0, teach), (1, learn)):
            enter.append(pltpu.make_async_copy(both_in.at[k, part], dst.at[part], sem.at[len(enter)]))
    enter.append(pltpu.make_async_copy(student_in.at[0], rows, sem.at[8]))
    enter.append(pltpu.make_async_copy(student_in.at[1], cols, sem.at[9]))
    for i in (0, 1, 9, 2, 3, 4, 5, 6, 7, 8):
        enter[i].start()
    row_st = merge([r[...] for r in (ra, rb, rc, rd)])
    col_st = merge([r[...] for r in (ca, cb)])
    row_t, row_s = row_st[0] + jnp.log(row_st[1]), row_st[2] + jnp.log(row_st[3])
    col_t, col_s = col_st[0] + jnp.log(col_st[1]), col_st[2] + jnp.log(col_st[3])
    part_r = jnp.sum(row_st[4] / row_st[1] + (row_s - row_t), axis=1, keepdims=True)
    part_c = jnp.sum(col_st[4] / col_st[1] + (col_s - col_t), axis=1, keepdims=True)
    loss_part[0] = jnp.broadcast_to(part_r, (8, LANES))
    loss_part[1] = jnp.broadcast_to(part_c, (8, LANES))
    whole = jnp.broadcast_to(part_r, (16, half))
    for k in range(3):
        piece = whole.astype(BF)
        give_text[16, 16 * k : 16 * k + 16] = piece
        whole = whole - piece.astype(F32)
    give_text[16, 48:] = jnp.zeros((n - 48, half), BF)
    for k, v in ((0, row_t), (1, row_s)):
        wide[k] = jnp.broadcast_to(v, (LANES, size)).T

    span = 4
    mine = pl.ds(pl.multiple_of(c * half, half), half)
    other = pl.ds(pl.multiple_of((1 - c) * half, half), half)

    def chunk_step(r, carry):
        part = pl.ds(pl.multiple_of(r * chunk, chunk), chunk)
        pltpu.make_async_copy(both_in.at[0, part], teach.at[part], sem.at[2 * r]).wait()
        pltpu.make_async_copy(both_in.at[1, part], learn.at[part], sem.at[2 * r + 1]).wait()
        for h in range(size // (span * LANES)):
            lanes = [slice((h * span + j) * LANES, (h * span + j + 1) * LANES) for j in range(span)]
            ct = [jnp.broadcast_to(col_t[:, s], (16, LANES)) for s in lanes]
            cs = [jnp.broadcast_to(col_s[:, s], (16, LANES)) for s in lanes]

            def step(i, inner):
                part = pl.ds(pl.multiple_of(r * chunk + i * 16, 16), 16)
                rt, rs = wide[0, part, :], wide[1, part, :]
                for j in range(span):
                    t, s = teach[part, lanes[j]], learn[part, lanes[j]]
                    v = jnp.exp(s - rs) - jnp.exp(t - rt) + jnp.exp(s - cs[j]) - jnp.exp(t - ct[j])
                    coupling[part, lanes[j]] = (0.5 * v).astype(BF)
                return inner

            lax.fori_loop(0, chunk // 16, step, 0, unroll=8)

        @pl.when(r == 0)
        def _():
            enter[9].wait()

        product[:chunk, :] = 100.0 * jnp.dot(
            coupling[part, :], cols[...].reshape(size, d), preferred_element_type=F32
        )
        for i in range(chunk // n):
            at = r * (chunk // n) + i
            dy = lax.rem(lax.div(at, NX) + NY - y, NY)
            dx = lax.rem(lax.rem(at, NX) + NX - x, NX)
            k = dy * (1 - c) + dx * c
            f = dx * (1 - c) + dy * c
            block = slice(i * n, (i + 1) * n)
            keep_image[f * 4 + k] = product[block, mine].astype(BF)
            give[k * 4 + f] = product[block, other].astype(BF)
        return carry

    lax.fori_loop(0, 4, chunk_step, 0)
    enter[8].wait()

    def text_step(i, carry):
        part = pl.ds(pl.multiple_of(i * 2 * chunk, 2 * chunk), 2 * chunk)
        product[part, :] = 100.0 * lax.dot_general(
            coupling[:, part],
            rows[...].reshape(size, d),
            (((0,), (0,)), ((), ())),
            preferred_element_type=F32,
        )
        return carry

    lax.fori_loop(0, 2, text_step, 0)
    out = 1 - 2 * c

    def text_block(k, core):
        at = lax.rem(z + NZ + k, NZ) * NC + core
        return product[pl.ds(pl.multiple_of(at * n, n), n), :]

    def put(i, v):
        v = v.astype(BF)
        give_text[i] = v[:, :half]
        give_text[8 + i] = v[:, half:]

    put(0, text_block(0, 1 - c))
    put(1, text_block(4, 1 - c))
    keep_text[0] = text_block(0, c)
    keep_text[1] = text_block(4, c)
    for k in (1, 2, 3):
        for core in range(2):
            put(2 * k + core, text_block(-out * k, core))
            keep_text[2 * k + core] = text_block(out * k, core)


def pass_2(args, n, d):
    size = NY * NX * n
    vmem = pl.BlockSpec(memory_space=pltpu.VMEM)
    return pl.pallas_call(
        pass_2_kernel,
        out_shape=(
            jax.ShapeDtypeStruct((16, n, d // 2), BF),
            jax.ShapeDtypeStruct((17, n, d // 2), BF),
            jax.ShapeDtypeStruct((16, n, d // 2), BF),
            jax.ShapeDtypeStruct((8, n, d), F32),
            jax.ShapeDtypeStruct((2, 8, LANES), F32),
        ),
        in_specs=[pl.BlockSpec(memory_space=pltpu.HBM)] * 2 + [vmem] * (len(args) - 2),
        out_specs=(vmem,) * 5,
        scratch_shapes=[
            pltpu.VMEM((size, size), F32),
            pltpu.VMEM((size, size), F32),
            pltpu.VMEM((16, n, d), BF),
            pltpu.VMEM((16, n, d), BF),
            pltpu.VMEM((size, size), BF),
            pltpu.VMEM((2, size, LANES), F32),
            pltpu.VMEM((size, d), F32),
            pltpu.SemaphoreType.DMA((10,)),
        ],
        compiler_params=pltpu.CompilerParams(vmem_limit_bytes=PASS_2_BYTES),
        cost_estimate=pl.CostEstimate(
            flops=4 * size * size * d, bytes_accessed=20 << 20, transcendentals=4 * size * size
        ),
    )(*args)


def vmem_call(kernel, outs, args):
    vmem = pl.BlockSpec(memory_space=pltpu.VMEM)
    return pl.pallas_call(
        kernel,
        out_shape=tuple(jax.ShapeDtypeStruct(s, t) for s, t in outs),
        in_specs=[vmem] * len(args),
        out_specs=(vmem,) * len(outs),
        compiler_params=pltpu.CompilerParams(vmem_limit_bytes=VMEM_BYTES),
        cost_estimate=pl.CostEstimate(flops=1 << 20, bytes_accessed=4 << 20, transcendentals=0),
    )(*args)


def pack(ref, row, lane, v):
    v = jnp.broadcast_to(v, (16, LANES))
    for k in range(3):
        piece = v.astype(BF)
        ref[row : row + 16, lane + k * LANES : lane + (k + 1) * LANES] = piece
        v = v - piece.astype(F32)


def unpack(ref, row, lane):
    v = ref[row : row + 16, lane : lane + 3 * LANES].astype(F32)
    return (v[:1, :LANES] + v[:1, LANES : 2 * LANES]) + v[:1, 2 * LANES :]


def choose(flag, a, b):
    return jnp.where(flag + jnp.zeros(a.shape, jnp.int32) == 0, a, b)


def load_text_kernel(keep_text, got, loss_part, text_own, k1, k2, k34, rows_loss):
    z, _, _, _ = position()
    n, h = got.shape[1:]
    for i in range(8):
        for q in range(2):
            lanes = slice(q * h, (q + 1) * h)
            v = keep_text[i, :, lanes] + got[8 * q + i].astype(F32)
            if i == 0:
                text_own[:, lanes] = v
            elif i == 1:
                k34[2 * n : 3 * n, lanes] = v.astype(BF)
            elif i >= 6:
                k34[(i - 6) * n : (i - 5) * n, lanes] = v.astype(BF)
            else:
                (k1, k2)[i // 2 - 1][i % 2, :, lanes] = v
    sib = got[16].astype(F32)
    chip = loss_part[0, :1] + ((sib[0:1, :LANES] + sib[16:17, :LANES]) + sib[32:33, :LANES])
    lane = lax.broadcasted_iota(jnp.int32, (1, LANES), 1)
    mine = jnp.where(lane == z, chip, 0.0)
    rows_loss[...] = jnp.broadcast_to(mine, (8, LANES))
    k34[3 * n :] = jnp.zeros((16, 2 * h), BF)
    pack(k34, 3 * n, 0, mine)


def load_image_kernel(keep_image, got, loss_part, image_own, p1, m1, far):
    n, h = got.shape[1:]
    image_own[0] = keep_image[0:4]
    image_own[1] = got[0:4]
    cols_loss = loss_part[1, :1]
    for f, out in ((1, p1), (2, far), (3, m1)):
        out[: 4 * n] = keep_image[f * 4 : f * 4 + 4].reshape(4 * n, h)
        out[4 * n : 8 * n] = got[f * 4 : f * 4 + 4].reshape(4 * n, h)
        out[8 * n :] = jnp.zeros((16, h), BF)
        pack(out, 8 * n, 0, cols_loss)


def pass_on_kernel(k1, k2, k34, rows_loss, b1, b2):
    _, c, _, _ = position()
    n, d = k1.shape[1:]
    for core in range(2):
        part = slice(core * n, (core + 1) * n)
        b1[part] = (k1[core] + k34[part].astype(F32)).astype(BF)
        v = k34[2 * n : 3 * n].astype(F32)
        b2[part] = (k2[core] + choose(c - core, v, jnp.zeros_like(v))).astype(BF)
    came = unpack(k34, 3 * n, 0)
    for ref in (b1, b2):
        ref[2 * n :] = jnp.zeros((16, d), BF)
    pack(b1, 2 * n, 0, rows_loss[:1] + came)
    pack(b2, 2 * n, 0, came)


def ring_sum(odd, own, back, ahead, far):
    return (own + choose(odd, ahead, back)) + (far + choose(odd, back, ahead))


def line_kernel(own, p1, m1, far, loss_part, out, w1, w2, w3, cols_loss):
    _, c, y, x = position()
    n, h = own.shape[2:]
    for k, ref in enumerate((out, w1, w2, w3)):
        for core in range(2):
            part = slice((core * 4 + k) * n, (core * 4 + k + 1) * n)
            v = own[core, k].astype(F32) + far[part].astype(F32)
            v = v + p1[part].astype(F32) + m1[part].astype(F32)
            ref[core * n : (core + 1) * n] = v.astype(ref.dtype)
    odd = lax.rem(x * (1 - c) + y * c, 2)
    v = ring_sum(odd, loss_part[1, :1], *[unpack(r, 8 * n, 0) for r in (p1, m1, far)])
    cols_loss[...] = jnp.broadcast_to(v, (8, LANES))
    for ref in (w1, w2, w3):
        ref[2 * n :] = jnp.zeros((16, h), BF)
        pack(ref, 2 * n, 0, v)


def last_kernel(
    text_own, b1, b2, k34, rows_loss, line, w1, w2, w3, cols_loss,
    text, image, share, loss,
):
    _, c, y, x = position()
    n, d = text.shape
    ways = []
    for core in range(2):
        part = slice(core * n, (core + 1) * n)
        ways.append(b1[part].astype(F32) + b2[part].astype(F32))
    text[...] = text_own[...] + choose(c, ways[0], ways[1])
    share[:n, :d] = choose(c, ways[1], ways[0]).astype(BF)
    v = line[...]
    for r in (w1, w2, w3):
        v = v + r[: 2 * n].astype(F32)
    image[...] = v[:n].astype(BF)
    share[:n, d:] = v[n:].astype(BF)
    odd = lax.rem(y * (1 - c) + x * c, 2)
    cols = ring_sum(odd, cols_loss[:1], *[unpack(r, 2 * n, 0) for r in (w1, w3, w2)])
    near = unpack(k34, 3 * n, 0) + unpack(b1, 2 * n, 0)
    rows = choose(c, near + (rows_loss[:1] + unpack(b2, 2 * n, 0)), near)
    share[n:] = jnp.zeros((16, share.shape[1]), BF)
    pack(share, n, 0, rows)
    pack(share, n, 3 * LANES, cols)
    loss[0] = jnp.broadcast_to(rows, (8, LANES))
    loss[1] = jnp.broadcast_to(cols, (8, LANES))


def end_kernel(scale, text, image, share, loss, text_grad, image_grad, total):
    _, c, _, _ = position()
    n, d = text.shape
    h = d // 2
    text_grad[...] = (text[...] + share[:n, :d].astype(F32)).astype(BF)
    mine, other = image[...].astype(F32), share[:n, d:].astype(F32)
    image_grad[:, :h] = choose(c, mine, other).astype(BF)
    image_grad[:, h:] = choose(c, other, mine).astype(BF)
    rows = loss[0, :1] + unpack(share, n, 0)
    cols = choose(c, loss[1, :1], unpack(share, n, 3 * LANES))
    total[0] = (jnp.sum(rows) + jnp.max(cols)) * scale


def reduce_all(give, give_text, keep_image, keep_text, loss_part):
    n, d = keep_text.shape[1:]
    h = d // 2
    small = ((8, LANES), F32)
    pair, line_out = ((2, n, d), F32), ((8 * n + 16, h), BF)
    text_own, k1, k2, k34, rows_loss = vmem_call(
        load_text_kernel,
        [((n, d), F32), pair, pair, ((3 * n + 16, d), BF), small],
        (keep_text, swap(give_text, c_bits=1), loss_part),
    )
    image_own, p1, m1, far = vmem_call(
        load_image_kernel,
        [((2, 4, n, h), BF)] + [line_out] * 3,
        (keep_image, swap(give, c_bits=1), loss_part),
    )
    far = move_first(far, 2)
    k34 = move_z(k34, 2)
    p1 = move_first(p1, 1)
    m1 = move_first(m1, -1)
    b1, b2 = vmem_call(
        pass_on_kernel, [((2 * n + 16, d), BF)] * 2, (k1, k2, k34, rows_loss)
    )
    b1 = move_z(b1, 1)
    b2 = move_z(b2, 2)
    line, w1, w2, w3, cols_loss = vmem_call(
        line_kernel,
        [((2 * n, h), F32)] + [((2 * n + 16, h), BF)] * 3 + [small],
        (image_own, p1, m1, far, loss_part),
    )
    w1 = move_second(w1, 1)
    w2 = move_second(w2, 2)
    w3 = move_second(w3, -1)
    text, image, share, loss = vmem_call(
        last_kernel,
        [((n, d), F32), ((n, h), BF), ((n + 16, d + h), BF), ((2, 8, LANES), F32)],
        (text_own, b1, b2, k34, rows_loss, line, w1, w2, w3, cols_loss),
    )
    vmem = pl.BlockSpec(memory_space=pltpu.VMEM)
    scale = 0.5 / (n * NX * NY * NZ * NC)
    return pl.pallas_call(
        functools.partial(end_kernel, scale),
        out_shape=(
            jax.ShapeDtypeStruct((n, d), BF),
            jax.ShapeDtypeStruct((n, d), BF),
            jax.ShapeDtypeStruct((1,), F32),
        ),
        in_specs=[vmem] * 4,
        out_specs=(vmem, vmem, pl.BlockSpec(memory_space=pltpu.SMEM)),
        compiler_params=pltpu.CompilerParams(vmem_limit_bytes=VMEM_BYTES),
    )(text, image, swap(share, c_bits=1), loss)


def merge_steps(row_st, col_st):
    row_st = merged([row_st] + [swap(row_st, x_bits=b) for b in (1, 2, 3)])
    col_st = merged([col_st] + [swap(col_st, z_bits=b) for b in (1, 2, 3)])
    row_parts = [row_st] + [swap(row_st, y_bits=b) for b in (1, 2, 3)]
    col_st = merged([col_st, swap(col_st, z_bits=4)])
    return row_parts + [col_st, swap(col_st, c_bits=1)]


def per_device(teacher_image, teacher_text, student_image, student_text):
    n, d = teacher_image.shape
    core = lax.rem(lax.axis_index("row"), NC)
    keep = jnp.where(core == 0, teacher_image, student_image)
    give = jnp.where(core == 0, student_image, teacher_image)
    texts = [teacher_text, student_text]
    texts = texts + [swap(v, c_bits=1) for v in texts]
    text = jnp.stack(texts).reshape(2, 2, n, d)
    text_blocks = gather_cols(text)
    image_blocks = gather_rows(jnp.stack([keep, swap(give, c_bits=1)]))
    both, student, row_st, col_st = pass_1(
        list(image_blocks) + list(text_blocks), n, d
    )
    give, give_text, keep_image, keep_text, loss_part = pass_2(
        [both, student] + merge_steps(row_st, col_st), n, d
    )
    text_grad, image_grad, loss = reduce_all(
        give, give_text, keep_image, keep_text, loss_part
    )
    return (image_grad, text_grad, loss.reshape(()))


def solution(mesh):
    placed = P(("row", "col"), None)
    return jax.shard_map(
        per_device,
        mesh=mesh,
        in_specs=(placed,) * 4,
        out_specs=(placed, placed, P()),
        check_vma=False,
    )
```

```python
import functools

import jax
import jax.numpy as jnp
from jax import lax
from jax.experimental import pallas as pl
from jax.experimental.pallas import tpu as pltpu
from jax.sharding import PartitionSpec as P

NX, NY, NZ, NC = 4, 4, 8, 2
BF = jnp.bfloat16
F32 = jnp.float32
GROUP = 8
LANES = 128
VMEM_BYTES = 16 << 20
PASS_1_BYTES = 40 << 20
PASS_2_BYTES = 48 << 20


def place(z, c, y, x):
    return ((z % NZ * NC + c) * NY + y % NY) * NX + x % NX


def send(v, target):
    pairs = [
        (place(z, c, y, x), place(*target(z, c, y, x)))
        for z in range(NZ)
        for c in range(NC)
        for y in range(NY)
        for x in range(NX)
    ]
    return lax.ppermute(v, ("row", "col"), pairs)


def swap(v, z_bits=0, c_bits=0, y_bits=0, x_bits=0):
    return send(v, lambda z, c, y, x: (z ^ z_bits, c ^ c_bits, y ^ y_bits, x ^ x_bits))


def move_first(v, d):
    return send(v, lambda z, c, y, x: (z, c, y + d * c, x + d * (1 - c)))


def move_second(v, d):
    return send(v, lambda z, c, y, x: (z, c, y + d * (1 - c), x + d * c))


def move_z(v, d):
    return send(v, lambda z, c, y, x: (z + d * (1 - 2 * c), c, y, x))


def position():
    row, col = lax.axis_index("row"), lax.axis_index("col")
    return lax.div(row, NC), lax.rem(row, NC), lax.div(col, NX), lax.rem(col, NX)


def gather_rows(v):
    from_m = move_first(v, 1)
    from_p = move_first(v, -1)
    from_2 = move_first(v, 2)
    line = jnp.stack([v, from_p, from_2, from_m], axis=1)
    up = move_second(line, 1)
    down = move_second(line, -1)
    far_a = move_second(up[:, :2], 1)
    far_b = move_second(down[:, 2:], -1)
    got_1 = swap(jnp.stack([line[1], down[1], up[1]]), c_bits=1)
    got_2 = swap(jnp.concatenate([far_a[1], far_b[1]]), c_bits=1)
    return line, up, down, far_a, far_b, got_1, got_2


def gather_cols(v):
    out = [v]
    for _ in range(3):
        out.append(move_z(out[-1], 1))
    far = move_z(out[3][0], 1)
    back = swap(jnp.stack(out[1:3]), c_bits=1)
    return out + [far, back, swap(out[3], c_bits=1), swap(far, c_bits=1)]


def pass_1_kernel(
    line, up, down, far_a, far_b, got_1, got_2,
    t0, t1, t2, t3, far, back, b3, far_sib,
    both_out, student, row_st, col_st,
    teach, learn, rows, cols, tops, wide, sums, sem,
):
    z, c, y, x = position()
    n, d = rows.shape[2:]
    size = teach.shape[0]
    tiles = size // LANES

    def row_place(second, first):
        dy = second * (1 - c) + first * c
        dx = first * (1 - c) + second * c
        return lax.rem(y + dy, NY) * NX + lax.rem(x + dx, NX)

    def col_place(steps, core):
        return lax.rem(z + NZ + steps, NZ) * NC + core

    pieces = []
    for k in range(4):
        for f in range(4):
            if k == 2:
                src = (far_a, (0, f)) if f < 2 else (far_b, (0, f - 2))
            else:
                src = ({0: line, 1: down, 3: up}[k], (0, f))
            pieces.append((src, (rows, c, row_place(k, f))))
            src = {0: (got_1, (0, k)), 1: (got_1, (1, k)), 2: (got_2, k), 3: (got_1, (2, k))}[f]
            pieces.append((src, (rows, 1 - c, row_place(k, f))))
    way = 2 * c - 1
    for kind in range(2):
        for j, ref in enumerate((t0, t1, t2, t3)):
            for dc in range(2):
                core = c if dc == 0 else 1 - c
                pieces.append(((ref, (dc, kind)), (cols, kind, col_place(way * j, core))))
        for j in range(3):
            for dc in range(2):
                core = 1 - c if dc == 0 else c
                src = (back, (j, dc, kind)) if j < 2 else (b3, (dc, kind))
                pieces.append((src, (cols, kind, col_place(-way * (j + 1), core))))
        pieces.append(((far, kind), (cols, kind, col_place(4, c))))
        pieces.append(((far_sib, kind), (cols, kind, col_place(4, 1 - c))))
    for (src, i), (dst, j, k) in pieces:
        dst[j, k] = src[i]
    leave = [
        pltpu.make_async_copy(rows.at[1], student.at[0], sem.at[0]),
        pltpu.make_async_copy(cols.at[1], student.at[1], sem.at[1]),
    ]
    for copy in leave:
        copy.start()

    for kind, buf in ((0, teach), (1, learn)):
        buf[...] = 100.0 * lax.dot_general(
            rows[kind].reshape(size, d),
            cols[kind].reshape(size, d),
            (((1,), (1,)), ((), ())),
            preferred_element_type=F32,
        )
        copy = pltpu.make_async_copy(buf, both_out.at[kind], sem.at[2 + kind])
        copy.start()
        leave.append(copy)

    def tile(ref, part, q):
        return ref[part, q * LANES : (q + 1) * LANES]

    def top_step(i, carry):
        part = pl.ds(pl.multiple_of(i * GROUP, GROUP), GROUP)
        out = []
        for k, ref in ((0, teach), (1, learn)):
            v = [tile(ref, part, q) for q in range(tiles)]
            out.append([jnp.maximum(a, b) for a, b in zip(carry[k], v)])
            while len(v) > 1:
                v = [jnp.maximum(a, b) for a, b in zip(v[::2], v[1::2])]
            tops[k, part, :] = v[0]
        return out

    low = jnp.full((GROUP, LANES), -jnp.inf, F32)
    col_tops = lax.fori_loop(0, size // GROUP, top_step, [[low] * tiles] * 2, unroll=4)
    col_tops = [[jnp.max(v, axis=0, keepdims=True) for v in tops_k] for tops_k in col_tops]
    row_tops = []
    for k in range(2):
        top = jnp.max(tops[k].T, axis=0, keepdims=True)
        row_tops.append(top)
        wide[k] = jnp.broadcast_to(top, (LANES, size)).T

    for h in range(2):
        span = range(h * tiles // 2, (h + 1) * tiles // 2)
        t_tops = [jnp.broadcast_to(col_tops[0][q], (GROUP, LANES)) for q in span]
        s_tops = [jnp.broadcast_to(col_tops[1][q], (GROUP, LANES)) for q in span]

        def sum_step(i, carry):
            part = pl.ds(pl.multiple_of(i * GROUP, GROUP), GROUP)
            rt, rs = wide[0, part, :], wide[1, part, :]
            acc = [0.0, 0.0, 0.0] if h == 0 else [sums[k, part, :] for k in range(3)]
            out = []
            for j, q in enumerate(span):
                t, s = tile(teach, part, q), tile(learn, part, q)
                gap = t - s
                e = jnp.exp(t - rt)
                acc = [acc[0] + e, acc[1] + jnp.exp(s - rs), acc[2] + e * gap]
                e = jnp.exp(t - t_tops[j])
                a, b, w = carry[j]
                out.append((a + e, b + jnp.exp(s - s_tops[j]), w + e * gap))
            for k in range(3):
                sums[k, part, :] = acc[k]
            return out

        none = jnp.zeros((GROUP, LANES), F32)
        out = lax.fori_loop(0, size // GROUP, sum_step, [(none,) * 3] * len(span), unroll=8)
        for j, q in enumerate(span):
            a, b, w = [jnp.sum(v, axis=0, keepdims=True) for v in out[j]]
            zero = jnp.zeros_like(w)
            col_st[:, q * LANES : (q + 1) * LANES] = jnp.concatenate(
                [col_tops[0][q], a, col_tops[1][q], b, w, zero, zero, zero], axis=0
            )
    a, b, w = [jnp.sum(sums[k].T, axis=0, keepdims=True) for k in range(3)]
    zero = jnp.zeros_like(w)
    row_st[...] = jnp.concatenate([row_tops[0], a, row_tops[1], b, w, zero, zero, zero], axis=0)
    for copy in leave:
        copy.wait()


def pass_1(pieces, n, d):
    size = NY * NX * n
    vmem = pl.BlockSpec(memory_space=pltpu.VMEM)
    hbm = pl.BlockSpec(memory_space=pltpu.HBM)
    both = jax.ShapeDtypeStruct((2, size, size), F32)
    blocks = jax.ShapeDtypeStruct((2, 16, n, d), BF)
    small = jax.ShapeDtypeStruct((8, size), F32)
    return pl.pallas_call(
        pass_1_kernel,
        out_shape=(both, blocks, small, small),
        in_specs=[vmem] * len(pieces),
        out_specs=(hbm, hbm, vmem, vmem),
        scratch_shapes=[
            pltpu.VMEM((size, size), F32),
            pltpu.VMEM((size, size), F32),
            pltpu.VMEM((2, 16, n, d), BF),
            pltpu.VMEM((2, 16, n, d), BF),
            pltpu.VMEM((2, size, LANES), F32),
            pltpu.VMEM((2, size, LANES), F32),
            pltpu.VMEM((3, size, LANES), F32),
            pltpu.SemaphoreType.DMA((4,)),
        ],
        compiler_params=pltpu.CompilerParams(vmem_limit_bytes=PASS_1_BYTES),
        cost_estimate=pl.CostEstimate(
            flops=4 * size * size * d, bytes_accessed=20 << 20, transcendentals=4 * size * size
        ),
    )(*pieces)


def merge(parts):
    parts = [[p[k : k + 1] for k in range(5)] for p in parts]
    t_top = parts[0][0]
    s_top = parts[0][2]
    for p in parts[1:]:
        t_top = jnp.maximum(t_top, p[0])
        s_top = jnp.maximum(s_top, p[2])
    terms = []
    for p in parts:
        a = jnp.exp(p[0] - t_top)
        terms.append((p[1] * a, p[3] * jnp.exp(p[2] - s_top), p[4] * a))
    while len(terms) > 1:
        terms = [
            tuple(u + v for u, v in zip(terms[i], terms[i + 1])) for i in range(0, len(terms), 2)
        ]
    t_sum, s_sum, w = terms[0]
    return [t_top, t_sum, s_top, s_sum, w]


def merged(parts):
    return jnp.concatenate(merge(parts), axis=0)


def pass_2_kernel(
    both_in, student_in, ra, rb, rc, rd, ca, cb,
    give, give_text, keep_image, keep_text, loss_part,
    teach, learn, rows, cols, coupling, wide, product, sem,
):
    z, c, y, x = position()
    n, d = rows.shape[1:]
    size = teach.shape[0]
    half = d // 2
    chunk = size // 4
    enter = []
    for r in range(4):
        part = pl.ds(r * chunk, chunk)
        for k, dst in ((0, teach), (1, learn)):
            enter.append(pltpu.make_async_copy(both_in.at[k, part], dst.at[part], sem.at[len(enter)]))
    enter.append(pltpu.make_async_copy(student_in.at[0], rows, sem.at[8]))
    enter.append(pltpu.make_async_copy(student_in.at[1], cols, sem.at[9]))
    for i in (0, 1, 9, 2, 3, 4, 5, 6, 7, 8):
        enter[i].start()
    row_st = merge([r[...] for r in (ra, rb, rc, rd)])
    col_st = merge([r[...] for r in (ca, cb)])
    row_t, row_s = row_st[0] + jnp.log(row_st[1]), row_st[2] + jnp.log(row_st[3])
    col_t, col_s = col_st[0] + jnp.log(col_st[1]), col_st[2] + jnp.log(col_st[3])
    part_r = jnp.sum(row_st[4] / row_st[1] + (row_s - row_t), axis=1, keepdims=True)
    part_c = jnp.sum(col_st[4] / col_st[1] + (col_s - col_t), axis=1, keepdims=True)
    loss_part[0] = jnp.broadcast_to(part_r, (8, LANES))
    loss_part[1] = jnp.broadcast_to(part_c, (8, LANES))
    whole = jnp.broadcast_to(part_r, (16, half))
    for k in range(3):
        piece = whole.astype(BF)
        give_text[16, 16 * k : 16 * k + 16] = piece
        whole = whole - piece.astype(F32)
    give_text[16, 48:] = jnp.zeros((n - 48, half), BF)
    for k, v in ((0, row_t), (1, row_s)):
        wide[k] = jnp.broadcast_to(v, (LANES, size)).T

    span = 4
    mine = pl.ds(pl.multiple_of(c * half, half), half)
    other = pl.ds(pl.multiple_of((1 - c) * half, half), half)

    def chunk_step(r, carry):
        part = pl.ds(pl.multiple_of(r * chunk, chunk), chunk)
        pltpu.make_async_copy(both_in.at[0, part], teach.at[part], sem.at[2 * r]).wait()
        pltpu.make_async_copy(both_in.at[1, part], learn.at[part], sem.at[2 * r + 1]).wait()
        for h in range(size // (span * LANES)):
            lanes = [slice((h * span + j) * LANES, (h * span + j + 1) * LANES) for j in range(span)]
            ct = [jnp.broadcast_to(col_t[:, s], (16, LANES)) for s in lanes]
            cs = [jnp.broadcast_to(col_s[:, s], (16, LANES)) for s in lanes]

            def step(i, inner):
                part = pl.ds(pl.multiple_of(r * chunk + i * 16, 16), 16)
                rt, rs = wide[0, part, :], wide[1, part, :]
                for j in range(span):
                    t, s = teach[part, lanes[j]], learn[part, lanes[j]]
                    v = jnp.exp(s - rs) - jnp.exp(t - rt) + jnp.exp(s - cs[j]) - jnp.exp(t - ct[j])
                    coupling[part, lanes[j]] = (0.5 * v).astype(BF)
                return inner

            lax.fori_loop(0, chunk // 16, step, 0, unroll=8)

        @pl.when(r == 0)
        def _():
            enter[9].wait()

        product[:chunk, :] = 100.0 * jnp.dot(
            coupling[part, :], cols[...].reshape(size, d), preferred_element_type=F32
        )
        for i in range(chunk // n):
            at = r * (chunk // n) + i
            dy = lax.rem(lax.div(at, NX) + NY - y, NY)
            dx = lax.rem(lax.rem(at, NX) + NX - x, NX)
            k = dy * (1 - c) + dx * c
            f = dx * (1 - c) + dy * c
            block = slice(i * n, (i + 1) * n)
            keep_image[f * 4 + k] = product[block, mine].astype(BF)
            give[k * 4 + f] = product[block, other].astype(BF)
        return carry

    lax.fori_loop(0, 4, chunk_step, 0)
    enter[8].wait()

    def text_step(i, carry):
        part = pl.ds(pl.multiple_of(i * 2 * chunk, 2 * chunk), 2 * chunk)
        product[part, :] = 100.0 * lax.dot_general(
            coupling[:, part],
            rows[...].reshape(size, d),
            (((0,), (0,)), ((), ())),
            preferred_element_type=F32,
        )
        return carry

    lax.fori_loop(0, 2, text_step, 0)
    out = 1 - 2 * c

    def text_block(k, core):
        at = lax.rem(z + NZ + k, NZ) * NC + core
        return product[pl.ds(pl.multiple_of(at * n, n), n), :]

    def put(i, v):
        v = v.astype(BF)
        give_text[i] = v[:, :half]
        give_text[8 + i] = v[:, half:]

    put(0, text_block(0, 1 - c))
    put(1, text_block(4, 1 - c))
    keep_text[0] = text_block(0, c)
    keep_text[1] = text_block(4, c)
    for k in (1, 2, 3):
        for core in range(2):
            put(2 * k + core, text_block(-out * k, core))
            keep_text[2 * k + core] = text_block(out * k, core)


def pass_2(args, n, d):
    size = NY * NX * n
    vmem = pl.BlockSpec(memory_space=pltpu.VMEM)
    return pl.pallas_call(
        pass_2_kernel,
        out_shape=(
            jax.ShapeDtypeStruct((16, n, d // 2), BF),
            jax.ShapeDtypeStruct((17, n, d // 2), BF),
            jax.ShapeDtypeStruct((16, n, d // 2), BF),
            jax.ShapeDtypeStruct((8, n, d), F32),
            jax.ShapeDtypeStruct((2, 8, LANES), F32),
        ),
        in_specs=[pl.BlockSpec(memory_space=pltpu.HBM)] * 2 + [vmem] * (len(args) - 2),
        out_specs=(vmem,) * 5,
        scratch_shapes=[
            pltpu.VMEM((size, size), F32),
            pltpu.VMEM((size, size), F32),
            pltpu.VMEM((16, n, d), BF),
            pltpu.VMEM((16, n, d), BF),
            pltpu.VMEM((size, size), BF),
            pltpu.VMEM((2, size, LANES), F32),
            pltpu.VMEM((size, d), F32),
            pltpu.SemaphoreType.DMA((10,)),
        ],
        compiler_params=pltpu.CompilerParams(vmem_limit_bytes=PASS_2_BYTES),
        cost_estimate=pl.CostEstimate(
            flops=4 * size * size * d, bytes_accessed=20 << 20, transcendentals=4 * size * size
        ),
    )(*args)


def vmem_call(kernel, outs, args):
    vmem = pl.BlockSpec(memory_space=pltpu.VMEM)
    return pl.pallas_call(
        kernel,
        out_shape=tuple(jax.ShapeDtypeStruct(s, t) for s, t in outs),
        in_specs=[vmem] * len(args),
        out_specs=(vmem,) * len(outs),
        compiler_params=pltpu.CompilerParams(vmem_limit_bytes=VMEM_BYTES),
        cost_estimate=pl.CostEstimate(flops=1 << 20, bytes_accessed=4 << 20, transcendentals=0),
    )(*args)


def pack(ref, row, lane, v):
    v = jnp.broadcast_to(v, (16, LANES))
    for k in range(3):
        piece = v.astype(BF)
        ref[row : row + 16, lane + k * LANES : lane + (k + 1) * LANES] = piece
        v = v - piece.astype(F32)


def unpack(ref, row, lane):
    v = ref[row : row + 16, lane : lane + 3 * LANES].astype(F32)
    return (v[:1, :LANES] + v[:1, LANES : 2 * LANES]) + v[:1, 2 * LANES :]


def choose(flag, a, b):
    return jnp.where(flag + jnp.zeros(a.shape, jnp.int32) == 0, a, b)


def load_text_kernel(keep_text, got, loss_part, text_own, k1, k2, k34, rows_loss):
    z, _, _, _ = position()
    n, h = got.shape[1:]
    for i in range(8):
        for q in range(2):
            lanes = slice(q * h, (q + 1) * h)
            v = keep_text[i, :, lanes] + got[8 * q + i].astype(F32)
            if i == 0:
                text_own[:, lanes] = v
            elif i == 1:
                k34[2 * n : 3 * n, lanes] = v.astype(BF)
            elif i >= 6:
                k34[(i - 6) * n : (i - 5) * n, lanes] = v.astype(BF)
            else:
                (k1, k2)[i // 2 - 1][i % 2, :, lanes] = v
    sib = got[16].astype(F32)
    chip = loss_part[0, :1] + ((sib[0:1, :LANES] + sib[16:17, :LANES]) + sib[32:33, :LANES])
    lane = lax.broadcasted_iota(jnp.int32, (1, LANES), 1)
    mine = jnp.where(lane == z, chip, 0.0)
    rows_loss[...] = jnp.broadcast_to(mine, (8, LANES))
    k34[3 * n :] = jnp.zeros((16, 2 * h), BF)
    pack(k34, 3 * n, 0, mine)


def load_image_kernel(keep_image, got, loss_part, image_own, p1, m1, far):
    n, h = got.shape[1:]
    image_own[0] = keep_image[0:4]
    image_own[1] = got[0:4]
    cols_loss = loss_part[1, :1]
    for f, out in ((1, p1), (2, far), (3, m1)):
        out[: 4 * n] = keep_image[f * 4 : f * 4 + 4].reshape(4 * n, h)
        out[4 * n : 8 * n] = got[f * 4 : f * 4 + 4].reshape(4 * n, h)
        out[8 * n :] = jnp.zeros((16, h), BF)
        pack(out, 8 * n, 0, cols_loss)


def pass_on_kernel(k1, k2, k34, rows_loss, b1, b2):
    _, c, _, _ = position()
    n, d = k1.shape[1:]
    for core in range(2):
        part = slice(core * n, (core + 1) * n)
        b1[part] = (k1[core] + k34[part].astype(F32)).astype(BF)
        v = k34[2 * n : 3 * n].astype(F32)
        b2[part] = (k2[core] + choose(c - core, v, jnp.zeros_like(v))).astype(BF)
    came = unpack(k34, 3 * n, 0)
    for ref in (b1, b2):
        ref[2 * n :] = jnp.zeros((16, d), BF)
    pack(b1, 2 * n, 0, rows_loss[:1] + came)
    pack(b2, 2 * n, 0, came)


def ring_sum(odd, own, back, ahead, far):
    return (own + choose(odd, ahead, back)) + (far + choose(odd, back, ahead))


def line_kernel(own, far, p1, m1, loss_part, out, w1, w2, w3, cols_loss):
    _, c, y, x = position()
    n, h = own.shape[2:]
    for k, ref in enumerate((out, w1, w2, w3)):
        for core in range(2):
            part = slice((core * 4 + k) * n, (core * 4 + k + 1) * n)
            v = own[core, k].astype(F32) + far[part].astype(F32)
            v = v + p1[part].astype(F32) + m1[part].astype(F32)
            ref[core * n : (core + 1) * n] = v.astype(ref.dtype)
    odd = lax.rem(x * (1 - c) + y * c, 2)
    v = ring_sum(odd, loss_part[1, :1], *[unpack(r, 8 * n, 0) for r in (p1, m1, far)])
    cols_loss[...] = jnp.broadcast_to(v, (8, LANES))
    for ref in (w1, w2, w3):
        ref[2 * n :] = jnp.zeros((16, h), BF)
        pack(ref, 2 * n, 0, v)


def last_kernel(
    text_own, b1, b2, k34, rows_loss, line, w2, w1, w3, cols_loss,
    text, image, share, loss,
):
    _, c, y, x = position()
    n, d = text.shape
    ways = []
    for core in range(2):
        part = slice(core * n, (core + 1) * n)
        ways.append(b1[part].astype(F32) + b2[part].astype(F32))
    text[...] = text_own[...] + choose(c, ways[0], ways[1])
    share[:n, :d] = choose(c, ways[1], ways[0]).astype(BF)
    v = line[...]
    for r in (w1, w2, w3):
        v = v + r[: 2 * n].astype(F32)
    image[...] = v[:n].astype(BF)
    share[:n, d:] = v[n:].astype(BF)
    odd = lax.rem(y * (1 - c) + x * c, 2)
    cols = ring_sum(odd, cols_loss[:1], *[unpack(r, 2 * n, 0) for r in (w1, w3, w2)])
    near = unpack(k34, 3 * n, 0) + unpack(b1, 2 * n, 0)
    rows = choose(c, near + (rows_loss[:1] + unpack(b2, 2 * n, 0)), near)
    share[n:] = jnp.zeros((16, share.shape[1]), BF)
    pack(share, n, 0, rows)
    pack(share, n, 3 * LANES, cols)
    loss[0] = jnp.broadcast_to(rows, (8, LANES))
    loss[1] = jnp.broadcast_to(cols, (8, LANES))


def end_kernel(scale, text, image, share, loss, text_grad, image_grad, total):
    _, c, _, _ = position()
    n, d = text.shape
    h = d // 2
    text_grad[...] = (text[...] + share[:n, :d].astype(F32)).astype(BF)
    mine, other = image[...].astype(F32), share[:n, d:].astype(F32)
    image_grad[:, :h] = choose(c, mine, other).astype(BF)
    image_grad[:, h:] = choose(c, other, mine).astype(BF)
    rows = loss[0, :1] + unpack(share, n, 0)
    cols = choose(c, loss[1, :1], unpack(share, n, 3 * LANES))
    total[0] = (jnp.sum(rows) + jnp.max(cols)) * scale


def reduce_all(give, give_text, keep_image, keep_text, loss_part):
    n, d = keep_text.shape[1:]
    h = d // 2
    small = ((8, LANES), F32)
    pair, line_out = ((2, n, d), F32), ((8 * n + 16, h), BF)
    text_own, k1, k2, k34, rows_loss = vmem_call(
        load_text_kernel,
        [((n, d), F32), pair, pair, ((3 * n + 16, d), BF), small],
        (keep_text, swap(give_text, c_bits=1), loss_part),
    )
    image_own, p1, m1, far = vmem_call(
        load_image_kernel,
        [((2, 4, n, h), BF)] + [line_out] * 3,
        (keep_image, swap(give, c_bits=1), loss_part),
    )
    far = move_first(far, 2)
    k34 = move_z(k34, 2)
    p1 = move_first(p1, 1)
    m1 = move_first(m1, -1)
    b1, b2 = vmem_call(
        pass_on_kernel, [((2 * n + 16, d), BF)] * 2, (k1, k2, k34, rows_loss)
    )
    b1 = move_z(b1, 1)
    b2 = move_z(b2, 2)
    line, w1, w2, w3, cols_loss = vmem_call(
        line_kernel,
        [((2 * n, h), F32)] + [((2 * n + 16, h), BF)] * 3 + [small],
        (image_own, far, p1, m1, loss_part),
    )
    w1 = move_second(w1, 1)
    w2 = move_second(w2, 2)
    w3 = move_second(w3, -1)
    text, image, share, loss = vmem_call(
        last_kernel,
        [((n, d), F32), ((n, h), BF), ((n + 16, d + h), BF), ((2, 8, LANES), F32)],
        (text_own, b1, b2, k34, rows_loss, line, w2, w1, w3, cols_loss),
    )
    vmem = pl.BlockSpec(memory_space=pltpu.VMEM)
    scale = 0.5 / (n * NX * NY * NZ * NC)
    return pl.pallas_call(
        functools.partial(end_kernel, scale),
        out_shape=(
            jax.ShapeDtypeStruct((n, d), BF),
            jax.ShapeDtypeStruct((n, d), BF),
            jax.ShapeDtypeStruct((1,), F32),
        ),
        in_specs=[vmem] * 4,
        out_specs=(vmem, vmem, pl.BlockSpec(memory_space=pltpu.SMEM)),
        compiler_params=pltpu.CompilerParams(vmem_limit_bytes=VMEM_BYTES),
    )(text, image, swap(share, c_bits=1), loss)


def merge_steps(row_st, col_st):
    row_st = merged([row_st] + [swap(row_st, x_bits=b) for b in (1, 2, 3)])
    col_st = merged([col_st] + [swap(col_st, z_bits=b) for b in (1, 2, 3)])
    row_parts = [row_st] + [swap(row_st, y_bits=b) for b in (1, 2, 3)]
    col_st = merged([col_st, swap(col_st, z_bits=4)])
    return row_parts + [col_st, swap(col_st, c_bits=1)]


def per_device(teacher_image, teacher_text, student_image, student_text):
    n, d = teacher_image.shape
    core = lax.rem(lax.axis_index("row"), NC)
    keep = jnp.where(core == 0, teacher_image, student_image)
    give = jnp.where(core == 0, student_image, teacher_image)
    texts = [teacher_text, student_text]
    texts = texts + [swap(v, c_bits=1) for v in texts]
    text = jnp.stack(texts).reshape(2, 2, n, d)
    text_blocks = gather_cols(text)
    image_blocks = gather_rows(jnp.stack([keep, swap(give, c_bits=1)]))
    both, student, row_st, col_st = pass_1(
        list(image_blocks) + list(text_blocks), n, d
    )
    give, give_text, keep_image, keep_text, loss_part = pass_2(
        [both, student] + merge_steps(row_st, col_st), n, d
    )
    text_grad, image_grad, loss = reduce_all(
        give, give_text, keep_image, keep_text, loss_part
    )
    return (image_grad, text_grad, loss.reshape(()))


def solution(mesh):
    placed = P(("row", "col"), None)
    return jax.shard_map(
        per_device,
        mesh=mesh,
        in_specs=(placed,) * 4,
        out_specs=(placed, placed, P()),
        check_vma=False,
    )
```
